512 devices in a mesh: blk: 32 (over y, x), row: 16 (over z, core).
Axes of the slice: x: 4, y: 8, z: 8, core: 2. Of those that a mesh axis runs over, the one named last changes fastest.
Arguments:
- snapshots: float32 [4096, 8192], P('row', 'blk'), may hold values from -20 to 20
Outputs:
- rotated: float32 [4096, 8192], P('row', 'blk')
The draws below stay inside these ranges and needn't reach their ends.
All inputs are finite; a program needn't handle non-finite values.
Results may differ from the reference program's by a relative error of at most 0.00027.
Values sent between devices are 32-bit elements; how exact they have to be, the bound alone decides.
A program may use at most 64 MiB of HBM per device.

```python
import math
import jax
import jax.numpy as jnp
from jax import lax

BW = 128
NSTEPS = 5
ROUNDS = 2
ROWS = 4096
COLS = 8192
N_BLK = 32


def draw_snapshots(key, part):
    key = jax.random.fold_in(key, 11)
    first_key, second_key = jax.random.split(key, 2)
    half_blocks = COLS // (2 * BW)
    base = jnp.clip(jax.random.normal(first_key, (ROWS, half_blocks, 2, BW), jnp.float32), -4.5, 4.5)
    mixed = base + 0.35 * base[:, :, ::-1, :]
    column_scale = jnp.exp(jax.random.uniform(second_key, (1, half_blocks, 2, BW), jnp.float32, math.log(0.3), math.log(3.0)))
    return (mixed * column_scale).reshape(ROWS, COLS)


def setup_inputs(seed: int = 0) -> dict:
    seeds = jax.random.split(jax.random.key(seed), 2)
    snapshots = draw_snapshots(jax.random.fold_in(seeds[1], 71), 0)
    return {"snapshots": snapshots}


def pair_update(column_pairs):
    pair_width = column_pairs.shape[2]
    gram = jnp.einsum('rkc,rkd->kcd', column_pairs, column_pairs, precision=lax.Precision.HIGHEST)
    diagonal = jnp.diagonal(gram, axis1=1, axis2=2)
    inverse_root = lax.rsqrt(diagonal)
    scaled = gram * inverse_root[:, :, None] * inverse_root[:, None, :]
    identity = jnp.eye(pair_width, dtype=jnp.float32)
    forward_it = 0.5 * scaled
    inverse_it = jnp.broadcast_to(identity, scaled.shape)
    for sweep_no in range(NSTEPS):
        factor = 1.5 * identity - 0.5 * jnp.einsum('kab,kbc->kac', inverse_it, forward_it, precision=lax.Precision.HIGHEST)
        forward_it = jnp.einsum('kab,kbc->kac', forward_it, factor, precision=lax.Precision.HIGHEST)
        inverse_it = jnp.einsum('kab,kbc->kac', factor, inverse_it, precision=lax.Precision.HIGHEST)
    rotation = inverse_root[:, :, None] * inverse_it * (math.sqrt(0.5) * jnp.sqrt(diagonal))[:, None, :]
    return jnp.einsum('rkc,kcd->rkd', column_pairs, rotation, precision=lax.Precision.HIGHEST)

def move_blocks(column_pairs):
    block_width = column_pairs.shape[2] // 2
    upper_half = column_pairs[:, :, :block_width]
    lower_half = column_pairs[:, :, block_width:]
    new_upper = jnp.concatenate([upper_half[:, 0:1], lower_half[:, 0:1], upper_half[:, 1:N_BLK - 1]], axis=1)
    new_lower = jnp.concatenate([lower_half[:, 1:], upper_half[:, N_BLK - 1:N_BLK]], axis=1)
    return jnp.concatenate([new_upper, new_lower], axis=2)

def reference(snapshots):
    column_pairs = snapshots.reshape(ROWS, N_BLK, 2 * BW)
    for round_no in range(ROUNDS):
        if round_no > 0:
            column_pairs = move_blocks(column_pairs)
        column_pairs = pair_update(column_pairs)
    return column_pairs.reshape(ROWS, COLS)
```

```python
import functools
import math

import jax
import jax.numpy as jnp
from jax import lax
from jax.experimental import pallas as pl
from jax.experimental.pallas import tpu as pltpu
from jax.sharding import PartitionSpec as P

NSTEPS = 5
MESH = pl.DeviceIdType.MESH


def product(a, b, lhs_dim=1):
    return lax.dot_general(
        a, b, (((lhs_dim,), (0,)), ((), ())), preferred_element_type=jnp.float32
    )


def split(a):
    high = a.astype(jnp.bfloat16)
    return high, (a - high.astype(jnp.float32)).astype(jnp.bfloat16)


def dot3(a, b, lhs_dim=1):
    return product(a[0], b[0], lhs_dim) + (
        product(a[0], b[1], lhs_dim) + product(a[1], b[0], lhs_dim)
    )


def eye(n):
    rows = lax.broadcasted_iota(jnp.int32, (n, n), 0)
    columns = lax.broadcasted_iota(jnp.int32, (n, n), 1)
    return rows == columns


def diagonals(a):
    kept = jnp.where(eye(a.shape[0]), a, 0.0)
    return jnp.sum(kept, axis=1, keepdims=True), jnp.sum(kept, axis=0, keepdims=True)


def newton_schulz(starts, last):
    n = starts[0].shape[0]
    scaled_eye = jnp.where(eye(n), 1.5, 0.0)
    ys = [split(0.5 * s) for s in starts]
    fs = [split(scaled_eye - 0.25 * s) for s in starts]
    zs = fs
    ys = [split(dot3(y, f)) for y, f in zip(ys, fs)]
    for step in range(1, NSTEPS):
        fs = [split(scaled_eye - 0.5 * dot3(z, y)) for z, y in zip(zs, ys)]
        if step == NSTEPS - 1:
            break
        ys, zs = (
            [split(dot3(y, f)) for y, f in zip(ys, fs)],
            [split(dot3(f, z)) for z, f in zip(zs, fs)],
        )
    return [last(n, f, y, z) for n, (f, y, z) in enumerate(zip(fs, ys, zs))]


def half_of(a, second, axis):
    n = a.shape[axis] // 2
    first = lax.slice_in_dim(a, 0, n, axis=axis)
    return jnp.where(second, lax.slice_in_dim(a, n, 2 * n, axis=axis), first)


def kernel(
    blk_devices, z_devices,
    x_ref, out_ref,
    moved, gram_local, gram_core, gram_sum, gram_parts, gram_shard, grams,
    cross_local, cross_core, cross_sum, cross_parts, cross_shard, cross,
    x_send, x_recv, gc_send, gc_recv, gz_send, gz_recv, ga_send, ga_recv, gf_send, gf_recv,
    cc_send, cc_recv, cz_send, cz_recv, ca_send, ca_recv, cf_send, cf_recv,
):
    k = lax.axis_index("blk")
    row = lax.axis_index("row")
    z = row // 2
    core = row % 2
    is_first = k == 0
    is_last = k == blk_devices - 1
    up = jnp.minimum(k + 1, blk_devices - 1)
    down = jnp.maximum(k - 1, 0)
    up_slot = jnp.where(is_last, 1, 0)
    down_slot = jnp.where(is_first, 0, 1)
    sibling = {"blk": k, "row": z * 2 + 1 - core}

    def peer(blk, t):
        return {"blk": blk, "row": lax.rem(z + t, z_devices) * 2 + core}

    def signal(device):
        pl.semaphore_signal(barrier, inc=1, device_id=device, device_id_type=MESH)

    def remote(src, dst, send, recv, device):
        return pltpu.make_async_remote_copy(
            src_ref=src, dst_ref=dst, send_sem=send, recv_sem=recv,
            device_id=device, device_id_type=MESH,
        )

    barrier = pltpu.get_barrier_semaphore()
    signal(sibling)
    for t in range(1, z_devices):
        signal(peer(k, t))

    @pl.when(jnp.logical_not(is_last))
    def _():
        for t in range(z_devices):
            signal(peer(up, t))

    @pl.when(jnp.logical_not(is_first))
    def _():
        for t in range(z_devices):
            signal(peer(down, t))

    x = x_ref[...]
    x_split = split(x)
    gram = dot3(x_split, x_split, 0)
    half_width = x.shape[1] // 2
    gram_local[:half_width] = gram[:half_width, :half_width]
    gram_local[half_width : 2 * half_width] = gram[:half_width, half_width:]
    gram_local[2 * half_width :] = gram[half_width:, half_width:]

    both = 1 - is_first.astype(jnp.int32) - is_last.astype(jnp.int32)
    pl.semaphore_wait(barrier, z_devices + z_devices + z_devices * both)

    g_half = gram_local.shape[0] // 2
    g_part = g_half // z_devices
    c_half = cross_local.shape[0] // 2
    c_part = c_half // z_devices

    def g_rows(which):
        return pl.ds(pl.multiple_of(which * g_half, 8), g_half)

    def c_rows(which):
        return pl.ds(pl.multiple_of(which * c_half, 8), c_half)

    gc = remote(gram_local.at[g_rows(1 - core)], gram_core, gc_send, gc_recv, sibling)
    gc.start()

    x_up = remote(x_ref, moved.at[up_slot], x_send.at[0], x_recv.at[up_slot], peer(up, 0))
    x_down = remote(x_ref, moved.at[down_slot], x_send.at[1], x_recv.at[down_slot], peer(down, 0))
    x_up_own = pltpu.make_async_copy(x_ref, moved.at[1], x_recv.at[1])
    x_down_own = pltpu.make_async_copy(x_ref, moved.at[0], x_recv.at[0])

    @pl.when(jnp.logical_not(is_last))
    def _():
        x_up.start()

    @pl.when(jnp.logical_not(is_first))
    def _():
        x_down.start()

    @pl.when(is_last)
    def _():
        x_up_own.start()

    @pl.when(is_first)
    def _():
        x_down_own.start()

    gc.wait_recv()
    gram_sum[...] = gram_local[g_rows(core)] + gram_core[...]

    gz = []
    for t in range(1, z_devices):
        there = lax.rem(z + t, z_devices)
        gz.append(
            remote(
                gram_sum.at[pl.ds(pl.multiple_of(there * g_part, 8), g_part)],
                gram_parts.at[t - 1], gz_send.at[t - 1], gz_recv.at[t - 1], peer(k, t),
            )
        )
        gz[-1].start()
    shard = gram_sum[pl.ds(pl.multiple_of(z * g_part, 8), g_part)]
    for t in range(1, z_devices):
        gz[t - 1].wait_recv()
        shard = shard + gram_parts[t - 1]
    gram_shard[...] = shard

    g_mine = pl.ds(pl.multiple_of(core * g_half + z * g_part, 8), g_part)
    ga_up = [
        remote(gram_shard, grams.at[up_slot, g_mine], ga_send.at[t], ga_recv.at[up_slot], peer(up, t))
        for t in range(z_devices)
    ]
    ga_down = [
        remote(
            gram_shard, grams.at[down_slot, g_mine],
            ga_send.at[z_devices + t], ga_recv.at[down_slot], peer(down, t),
        )
        for t in range(z_devices)
    ]
    ga_up_own = pltpu.make_async_copy(gram_shard, grams.at[1, g_mine], ga_recv.at[1])
    ga_down_own = pltpu.make_async_copy(gram_shard, grams.at[0, g_mine], ga_recv.at[0])

    @pl.when(jnp.logical_not(is_last))
    def _():
        ga_up[0].start()

    @pl.when(jnp.logical_not(is_first))
    def _():
        ga_down[0].start()

    @pl.when(is_last)
    def _():
        ga_up_own.start()

    @pl.when(is_first)
    def _():
        ga_down_own.start()

    for t in range(1, z_devices):
        ga_up[t].start()
        ga_down[t].start()

    for slot in range(2):
        pltpu.make_async_copy(moved.at[slot], moved.at[slot], x_recv.at[slot]).wait()
    a_split = split(moved[0])
    b_split = split(moved[1])
    cross_local[...] = dot3(a_split, b_split, 0)
    cc = remote(cross_local.at[c_rows(1 - core)], cross_core, cc_send, cc_recv, sibling)
    cc.start()
    cc.wait_recv()
    cross_sum[...] = cross_local[c_rows(core)] + cross_core[...]
    cz = []
    for t in range(1, z_devices):
        there = lax.rem(z + t, z_devices)
        cz.append(
            remote(
                cross_sum.at[pl.ds(pl.multiple_of(there * c_part, 8), c_part)],
                cross_parts.at[t - 1], cz_send.at[t - 1], cz_recv.at[t - 1], peer(k, t),
            )
        )
        cz[-1].start()

    gf = []
    for slot in range(2):
        here = grams.at[slot, g_rows(core)]
        pltpu.make_async_copy(here, here, ga_recv.at[slot]).wait()
        gf.append(remote(here, here, gf_send.at[slot], gf_recv.at[slot], sibling))
        gf[-1].start()

    shard = cross_sum[pl.ds(pl.multiple_of(z * c_part, 8), c_part)]
    for t in range(1, z_devices):
        cz[t - 1].wait_recv()
        shard = shard + cross_parts[t - 1]
    cross_shard[...] = shard
    c_mine = pl.ds(pl.multiple_of(core * c_half + z * c_part, 8), c_part)
    ca = []
    for t in range(1, z_devices):
        ca.append(
            remote(cross_shard, cross.at[c_mine], ca_send.at[t - 1], ca_recv.at[0], peer(k, t))
        )
        ca[-1].start()
    ca_own = pltpu.make_async_copy(cross_shard, cross.at[c_mine], ca_recv.at[0])
    ca_own.start()

    for slot in range(2):
        gf[slot].wait_recv()

    second = (k == 1, jnp.logical_not(is_last))
    diag_columns, diag_rows, roots_columns, scaled = [], [], [], []
    for slot in range(2):
        g = grams[slot]
        upper = g[half_width : 2 * half_width]
        full = jnp.concatenate(
            [
                jnp.concatenate([g[:half_width], upper], axis=1),
                jnp.concatenate([upper.T, g[2 * half_width :]], axis=1),
            ],
            axis=0,
        )
        column, line = diagonals(full)
        diag_columns.append(column)
        diag_rows.append(line)
        roots_columns.append(lax.rsqrt(column))
        scaled.append(full * roots_columns[slot] * lax.rsqrt(line))
    scaled_split = [split(s) for s in scaled]

    def end_first(slot, factor, y, z_now):
        z_half = [half_of(part.astype(jnp.float32), second[slot], 1).astype(jnp.bfloat16) for part in z_now]
        return dot3(factor, z_half)

    z_first = newton_schulz(scaled, end_first)
    z_split = [split(v) for v in z_first]
    own = [dot3(z_split[s], split(dot3(scaled_split[s], z_split[s])), 0) for s in range(2)]

    here = cross.at[c_rows(core)]
    pltpu.make_async_copy(here, here, ca_recv.at[0]).wait()
    cf = remote(here, here, cf_send, cf_recv, sibling)
    cf.start()
    cf.wait_recv()

    cross_scaled = cross[...] * roots_columns[0] * lax.rsqrt(diag_rows[1])
    between = dot3(z_split[0], split(dot3(split(cross_scaled), z_split[1])), 0)
    t_columns, t_rows = zip(*[diagonals(o) for o in own])
    it_columns = [lax.rsqrt(v) for v in t_columns]
    it_rows = [lax.rsqrt(v) for v in t_rows]
    off = between * it_columns[0] * it_rows[1]
    scaled2 = jnp.concatenate(
        [
            jnp.concatenate([own[0] * it_columns[0] * it_rows[0], off], axis=1),
            jnp.concatenate([off.T, own[1] * it_columns[1] * it_rows[1]], axis=1),
        ],
        axis=0,
    )
    (z_second,) = newton_schulz([scaled2], lambda n, factor, y, z_now: dot3(factor, z_now))

    diag2 = jnp.concatenate(
        [half_of(diag_rows[s], second[s], 1) * t_rows[s] for s in range(2)], axis=1
    )
    ends = math.sqrt(0.5) * jnp.sqrt(0.5 * diag2)
    result = None
    for s in range(2):
        mine = z_second[s * half_width : (s + 1) * half_width] * it_columns[s]
        both_rotations = roots_columns[s] * dot3(z_split[s], split(mine)) * ends
        term = dot3((a_split, b_split)[s], split(both_rotations))
        result = term if result is None else result + term
    out_ref[...] = result

    gc.wait_send()
    cc.wait_send()
    cf.wait_send()
    for copy in gz + cz + ca + gf + ga_up[1:] + ga_down[1:]:
        copy.wait_send()

    @pl.when(jnp.logical_not(is_last))
    def _():
        x_up.wait_send()
        ga_up[0].wait_send()

    @pl.when(jnp.logical_not(is_first))
    def _():
        x_down.wait_send()
        ga_down[0].wait_send()


def shards(blk_devices, z_devices, x):
    rows, width = x.shape
    half = width // 2
    dma = pltpu.SemaphoreType.DMA
    f32 = jnp.float32
    g_half, c_half = 3 * half // 2, width // 2
    vmem = pl.BlockSpec(memory_space=pltpu.VMEM)
    return pl.pallas_call(
        functools.partial(kernel, blk_devices, z_devices),
        out_shape=jax.ShapeDtypeStruct(x.shape, f32),
        in_specs=[vmem],
        out_specs=vmem,
        scratch_shapes=[
            pltpu.VMEM((2, rows, width), f32),
            pltpu.VMEM((3 * half, half), f32),
            pltpu.VMEM((g_half, half), f32),
            pltpu.VMEM((g_half, half), f32),
            pltpu.VMEM((z_devices - 1, g_half // z_devices, half), f32),
            pltpu.VMEM((g_half // z_devices, half), f32),
            pltpu.VMEM((2, 3 * half, half), f32),
            pltpu.VMEM((width, width), f32),
            pltpu.VMEM((c_half, width), f32),
            pltpu.VMEM((c_half, width), f32),
            pltpu.VMEM((z_devices - 1, c_half // z_devices, width), f32),
            pltpu.VMEM((c_half // z_devices, width), f32),
            pltpu.VMEM((width, width), f32),
            dma((2,)), dma((2,)), dma, dma,
            dma((z_devices - 1,)), dma((z_devices - 1,)), dma((2 * z_devices,)), dma((2,)),
            dma((2,)), dma((2,)), dma, dma,
            dma((z_devices - 1,)), dma((z_devices - 1,)), dma((z_devices - 1,)), dma((1,)),
            dma, dma,
        ],
        compiler_params=pltpu.CompilerParams(
            collective_id=0, has_side_effects=True, vmem_limit_bytes=32 * 1024 * 1024
        ),
        cost_estimate=pl.CostEstimate(
            flops=40 * 3 * 2 * width**3, bytes_accessed=8 * rows * width, transcendentals=4096
        ),
        name="rotate_pairs",
    )(x)


def solution(mesh):
    run = functools.partial(shards, mesh.shape["blk"], mesh.shape["row"] // 2)
    return jax.shard_map(
        run, mesh=mesh, in_specs=(P("row", "blk"),), out_specs=P("row", "blk"), check_vma=False
    )
```

```python
import functools
import math

import jax
import jax.numpy as jnp
from jax import lax
from jax.experimental import pallas as pl
from jax.experimental.pallas import tpu as pltpu
from jax.sharding import PartitionSpec as P

NSTEPS = 5
MESH = pl.DeviceIdType.MESH


def product(a, b, lhs_dim=1):
    return lax.dot_general(
        a, b, (((lhs_dim,), (0,)), ((), ())), preferred_element_type=jnp.float32
    )


def split(a):
    high = a.astype(jnp.bfloat16)
    return high, (a - high.astype(jnp.float32)).astype(jnp.bfloat16)


def dot3(a, b, lhs_dim=1):
    return product(a[0], b[0], lhs_dim) + (
        product(a[0], b[1], lhs_dim) + product(a[1], b[0], lhs_dim)
    )


def eye(n):
    rows = lax.broadcasted_iota(jnp.int32, (n, n), 0)
    columns = lax.broadcasted_iota(jnp.int32, (n, n), 1)
    return rows == columns


def diagonals(a):
    kept = jnp.where(eye(a.shape[0]), a, 0.0)
    return jnp.sum(kept, axis=1, keepdims=True), jnp.sum(kept, axis=0, keepdims=True)


class Solve:
    def __init__(self, starts):
        self.eye = jnp.where(eye(starts[0].shape[0]), 1.5, 0.0)
        self.f = [split(self.eye - 0.25 * m) for m in starts]
        self.y = [dot3(split(0.5 * m), f) for m, f in zip(starts, self.f)]
        self.z = [self.eye - 0.25 * m for m in starts]
        self.z_split = self.f
        self.y_split = [split(y) for y in self.y]

    def factors(self):
        self.f = [split(self.eye - 0.5 * dot3(z, y)) for z, y in zip(self.z_split, self.y_split)]

    def step(self):
        self.factors()
        self.y = [dot3(y, f) for y, f in zip(self.y_split, self.f)]
        self.z = [dot3(f, z) for z, f in zip(self.z_split, self.f)]
        self.y_split = [split(y) for y in self.y]
        self.z_split = [split(z) for z in self.z]


def half_of(a, second, axis):
    n = a.shape[axis] // 2
    first = lax.slice_in_dim(a, 0, n, axis=axis)
    return jnp.where(second, lax.slice_in_dim(a, n, 2 * n, axis=axis), first)


def kernel(
    blk_devices, z_devices,
    x_hbm, out_ref,
    x_ref, moved, gram_local, gram_core, gram_sum, gram_parts, gram_full, grams,
    cross_local, cross_core, cross_sum, cross_parts, cross_shard, cross,
    load_sem, x_send, x_recv, gc_send, gc_recv, gz_send, gz_recv, ga_send, ga_recv, gx_send, gx_recv,
    cc_send, cc_recv, cz_send, cz_recv, ca_send, ca_recv, cf_send, cf_recv,
):
    k = lax.axis_index("blk")
    row = lax.axis_index("row")
    z = row // 2
    core = row % 2
    is_first = k == 0
    is_last = k == blk_devices - 1
    up = jnp.minimum(k + 1, blk_devices - 1)
    down = jnp.maximum(k - 1, 0)
    up_slot = jnp.where(is_last, 1, 0)
    down_slot = jnp.where(is_first, 0, 1)
    second = (k == 1, jnp.logical_not(is_last))
    half_width = x_ref.shape[1] // 2
    g_half = gram_local.shape[0] // 2
    g_part = g_half // z_devices
    c_half = cross_local.shape[0] // 2
    c_part = c_half // z_devices
    far_first = sorted(range(1, z_devices), key=lambda t: -min(t, z_devices - t))
    near_first = far_first[::-1]

    def peer(blk, t, other=False):
        return {"blk": blk, "row": lax.rem(z + t, z_devices) * 2 + (1 - core if other else core)}

    sibling = peer(k, 0, True)

    def remote(src, dst, send, recv, device):
        return pltpu.make_async_remote_copy(
            src_ref=src, dst_ref=dst, send_sem=send, recv_sem=recv,
            device_id=device, device_id_type=MESH,
        )

    def rows_at(start, size):
        return pl.ds(pl.multiple_of(start, 8), size)

    def either(condition, yes, no):
        pl.when(condition)(lambda: yes() and None)
        pl.when(jnp.logical_not(condition))(lambda: no() and None)

    load = pltpu.make_async_copy(x_hbm, x_ref, load_sem)
    load.start()

    barrier = pltpu.get_barrier_semaphore()

    def signal(device):
        pl.semaphore_signal(barrier, inc=1, device_id=device, device_id_type=MESH)

    for t in far_first:
        signal(peer(k, t))

    @pl.when(jnp.logical_not(is_last))
    def _():
        signal(peer(up, 0))
        signal(peer(up, 0, True))

    @pl.when(jnp.logical_not(is_first))
    def _():
        signal(peer(down, 0))
        signal(peer(down, 0, True))

    signal(sibling)

    load.wait()
    x_split = split(x_ref[...])
    g = dot3(x_split, x_split, 0)
    gram_local[:half_width] = g[:half_width, :half_width]
    gram_local[half_width : 2 * half_width] = g[:half_width, half_width:]
    gram_local[2 * half_width :] = g[half_width:, half_width:]

    neighbours = 2 - is_first.astype(jnp.int32) - is_last.astype(jnp.int32)
    pl.semaphore_wait(barrier, z_devices + 2 * neighbours)

    x_up = remote(x_ref, moved.at[up_slot], x_send.at[0], x_recv.at[up_slot], peer(up, 0))
    x_down = remote(x_ref, moved.at[down_slot], x_send.at[1], x_recv.at[down_slot], peer(down, 0))
    either(is_last, pltpu.make_async_copy(x_ref, moved.at[1], x_recv.at[1]).start, x_up.start)
    either(is_first, pltpu.make_async_copy(x_ref, moved.at[0], x_recv.at[0]).start, x_down.start)

    gc = remote(gram_local.at[rows_at((1 - core) * g_half, g_half)], gram_core, gc_send, gc_recv, sibling)
    gc.start()
    sent = [gc]

    def scatter(total, part, parts, send, recv):
        copies = {}
        for t in far_first:
            there = rows_at(lax.rem(z + t, z_devices) * part, part)
            copies[t] = remote(total.at[there], parts.at[t - 1], send.at[t - 1], recv.at[t - 1], peer(k, t))
            copies[t].start()
        sent.extend(copies.values())
        return copies

    def gather(total, part, parts, copies):
        shard = total[rows_at(z * part, part)]
        for t in near_first:
            copies[t].wait_recv()
            shard = shard + parts[t - 1]
        return shard

    gc.wait_recv()
    gram_sum[...] = gram_local[rows_at(core * g_half, g_half)] + gram_core[...]
    gz = scatter(gram_sum, g_part, gram_parts, gz_send, gz_recv)
    own_rows = rows_at(z * g_part, g_part)
    gram_full[own_rows] = gather(gram_sum, g_part, gram_parts, gz)
    ga = {}
    for t in far_first:
        ga[t] = remote(
            gram_full.at[own_rows], gram_full.at[own_rows], ga_send.at[t - 1], ga_recv.at[t - 1], peer(k, t)
        )
        ga[t].start()
    sent.extend(ga.values())

    forwarded = []

    def forward(t):
        from_z = lax.rem(z - t + z_devices, z_devices)
        src = gram_full.at[rows_at(from_z * g_part, g_part)]
        there = rows_at(core * g_half + from_z * g_part, g_part)
        if t:
            ga[t].wait_recv()
        for n, (edge, blk, slot, own_slot) in enumerate(((is_last, up, up_slot, 1), (is_first, down, down_slot, 0))):
            dst = grams.at[slot, there]
            straight = remote(src, dst, gx_send.at[2 * n, t], gx_recv.at[slot], peer(blk, 0))
            across = remote(src, dst, gx_send.at[2 * n + 1, t], gx_recv.at[slot], peer(blk, 0, True))
            stays = pltpu.make_async_copy(src, grams.at[own_slot, there], gx_recv.at[own_slot])
            across.start()
            either(edge, stays.start, straight.start)
            sent.append(across)
            forwarded.append((edge, straight))

    forward(0)

    for slot in range(2):
        pltpu.make_async_copy(moved.at[slot], moved.at[slot], x_recv.at[slot]).wait()
    moved_split = [split(moved[slot]) for slot in range(2)]
    cross_local[...] = dot3(*moved_split, 0)
    cc = remote(cross_local.at[rows_at((1 - core) * c_half, c_half)], cross_core, cc_send, cc_recv, sibling)
    cc.start()
    sent.append(cc)
    for t in near_first[:2]:
        forward(t)
    cc.wait_recv()
    cross_sum[...] = cross_local[rows_at(core * c_half, c_half)] + cross_core[...]
    cz = scatter(cross_sum, c_part, cross_parts, cz_send, cz_recv)
    for t in near_first[2:]:
        forward(t)

    for slot in range(2):
        pltpu.make_async_copy(grams.at[slot], grams.at[slot], gx_recv.at[slot]).wait()
    diag_rows, roots_columns, scaled = [], [], []
    for slot in range(2):
        g = grams[slot]
        upper = g[half_width : 2 * half_width]
        full = jnp.concatenate(
            [
                jnp.concatenate([g[:half_width], upper], axis=1),
                jnp.concatenate([upper.T, g[2 * half_width :]], axis=1),
            ],
            axis=0,
        )
        column, line = diagonals(full)
        diag_rows.append(line)
        roots_columns.append(lax.rsqrt(column))
        scaled.append(full * roots_columns[slot] * lax.rsqrt(line))
    first = Solve(scaled)
    first.step()

    cross_shard[...] = gather(cross_sum, c_part, cross_parts, cz)
    c_mine = rows_at(core * c_half + z * c_part, c_part)
    for t in far_first:
        ca = remote(cross_shard, cross.at[c_mine], ca_send.at[t - 1], ca_recv, peer(k, t))
        ca.start()
        sent.append(ca)
    pltpu.make_async_copy(cross_shard, cross.at[c_mine], ca_recv).start()

    for _ in range(NSTEPS - 3):
        first.step()
    first.factors()
    zs, t_rows, its, ul = [], [], [], []
    for n in range(2):
        z_half = dot3(first.f[n], split(half_of(first.z[n], second[n], 1)))
        y_half = dot3(first.f[n], split(half_of(first.y[n], second[n], 1)))
        own = 2.0 * dot3(split(z_half), split(y_half), 0)
        t_column, t_row = diagonals(own)
        it_row = lax.rsqrt(t_row)
        t_rows.append(t_row)
        z_unit = z_half * it_row
        zs.append(split(z_unit))
        its.append(own * lax.rsqrt(t_column) * it_row)
        ul.append(split(dot3(moved_split[n], split(z_unit * roots_columns[n]))))
    ul = [jnp.concatenate([ul[0][p], ul[1][p]], axis=1) for p in range(2)]
    diag2 = jnp.concatenate([half_of(diag_rows[n], second[n], 1) * t_rows[n] for n in range(2)], axis=1)
    ends = math.sqrt(0.5) * jnp.sqrt(0.5 * diag2)
    root_row = lax.rsqrt(diag_rows[1])

    here = cross.at[rows_at(core * c_half, c_half)]
    pltpu.make_async_copy(here, here, ca_recv).wait()
    cf = remote(here, here, cf_send, cf_recv, sibling)
    cf.start()
    sent.append(cf)
    cf.wait_recv()

    cross_scaled = cross[...] * roots_columns[0] * root_row
    off = dot3(zs[0], split(dot3(split(cross_scaled), zs[1])), 0)
    scaled2 = jnp.concatenate(
        [jnp.concatenate([its[0], off], axis=1), jnp.concatenate([off.T, its[1]], axis=1)], axis=0
    )
    last = Solve([scaled2])
    for _ in range(NSTEPS - 2):
        last.step()
    last.factors()
    almost = dot3(ul, last.z_split[0])
    out_ref[...] = dot3(split(almost), last.f[0]) * ends

    for copy in sent:
        copy.wait_send()
    for edge, copy in forwarded + [(is_last, x_up), (is_first, x_down)]:
        pl.when(jnp.logical_not(edge))(lambda copy=copy: copy.wait_send())


def shards(blk_devices, z_devices, x):
    rows, width = x.shape
    half = width // 2
    dma = pltpu.SemaphoreType.DMA
    g_half, c_half = 3 * half // 2, width // 2
    others = z_devices - 1
    vmem = lambda *shape: pltpu.VMEM(shape, jnp.float32)
    return pl.pallas_call(
        functools.partial(kernel, blk_devices, z_devices),
        out_shape=jax.ShapeDtypeStruct(x.shape, jnp.float32),
        in_specs=[pl.BlockSpec(memory_space=pltpu.MemorySpace.HBM)],
        out_specs=pl.BlockSpec(memory_space=pltpu.VMEM),
        scratch_shapes=[
            vmem(rows, width), vmem(2, rows, width),
            vmem(3 * half, half), vmem(g_half, half), vmem(g_half, half),
            vmem(others, g_half // z_devices, half), vmem(g_half, half), vmem(2, 3 * half, half),
            vmem(width, width), vmem(c_half, width), vmem(c_half, width),
            vmem(others, c_half // z_devices, width), vmem(c_half // z_devices, width), vmem(width, width),
            dma, dma((2,)), dma((2,)), dma, dma,
            dma((others,)), dma((others,)), dma((others,)), dma((others,)), dma((4, z_devices)), dma((2,)),
            dma, dma, dma((others,)), dma((others,)), dma((others,)), dma, dma, dma,
        ],
        compiler_params=pltpu.CompilerParams(
            collective_id=0, has_side_effects=True, vmem_limit_bytes=32 * 1024 * 1024
        ),
        cost_estimate=pl.CostEstimate(
            flops=40 * 3 * 2 * width**3, bytes_accessed=8 * rows * width, transcendentals=4096
        ),
        name="rotate_pairs",
    )(pltpu.with_memory_space_constraint(x, pltpu.MemorySpace.HBM))


def solution(mesh):
    run = functools.partial(shards, mesh.shape["blk"], mesh.shape["row"] // 2)
    return jax.shard_map(
        run, mesh=mesh, in_specs=(P("row", "blk"),), out_specs=P("row", "blk"), check_vma=False
    )
```

```python
import functools
import math

import jax
import jax.numpy as jnp
from jax import lax
from jax.experimental import pallas as pl
from jax.experimental.pallas import tpu as pltpu
from jax.sharding import PartitionSpec as P

NSTEPS = 5
MESH = pl.DeviceIdType.MESH


def product(a, b, lhs_dim=1):
    return lax.dot_general(
        a, b, (((lhs_dim,), (0,)), ((), ())), preferred_element_type=jnp.float32
    )


def split(a):
    high = a.astype(jnp.bfloat16)
    return high, (a - high.astype(jnp.float32)).astype(jnp.bfloat16)


def dot3(a, b, lhs_dim=1):
    high, low = a
    if lhs_dim == 0:
        return product(high, b[0], 0) + (product(high, b[1], 0) + product(low, b[0], 0))
    half = high.shape[0] // 2
    blocks = []
    for rows in (slice(0, half), slice(half, 2 * half)):
        small = product(high[rows], b[1]) + product(low[rows], b[0])
        blocks.append(product(high[rows], b[0]) + small)
    return jnp.concatenate(blocks, axis=0)


def eye(n):
    rows = lax.broadcasted_iota(jnp.int32, (n, n), 0)
    columns = lax.broadcasted_iota(jnp.int32, (n, n), 1)
    return rows == columns


def diagonals(a):
    kept = jnp.where(eye(a.shape[0]), a, 0.0)
    return jnp.sum(kept, axis=1, keepdims=True), jnp.sum(kept, axis=0, keepdims=True)


class Solve:
    def __init__(self, starts):
        self.eye = jnp.where(eye(starts[0].shape[0]), 1.5, 0.0)
        y = [0.25 * m for m in starts]
        self.z = [self.eye - m for m in y]
        self.f = self.z_split = [split(z) for z in self.z]
        self.y = [dot3(f, split(m)) for f, m in zip(self.f, y)]
        self.y_split = [split(m) for m in self.y]

    def factors(self):
        self.f = [split(self.eye - dot3(y, z)) for y, z in zip(self.y_split, self.z_split)]

    def step(self):
        self.factors()
        self.z = [dot3(f, z) for f, z in zip(self.f, self.z_split)]
        self.z_split = [split(z) for z in self.z]
        self.y = [dot3(f, y) for f, y in zip(self.f, self.y_split)]
        self.y_split = [split(y) for y in self.y]


def half_of(a, second, axis):
    n = a.shape[axis] // 2
    first = lax.slice_in_dim(a, 0, n, axis=axis)
    return jnp.where(second, lax.slice_in_dim(a, n, 2 * n, axis=axis), first)


def kernel(
    blk_devices, z_devices,
    x_hbm, out_ref,
    x_ref, moved, gram_local, gram_core, gram_sum, gram_parts, gram_full, grams,
    cross_local, cross_core, cross_sum, cross_parts, cross_shard, cross,
    here_sem, load_sem, x_send, x_recv, gc_send, gc_recv, gz_send, gz_recv, ga_send, ga_recv,
    straight_send, across_send, gx_recv, cc_send, cc_recv, cz_send, cz_recv, ca_send, ca_recv, cf_send, cf_recv,
):
    k = lax.axis_index("blk")
    row = lax.axis_index("row")
    z = row // 2
    core = row % 2
    is_first = k == 0
    is_last = k == blk_devices - 1
    up = jnp.minimum(k + 1, blk_devices - 1)
    down = jnp.maximum(k - 1, 0)
    up_slot = jnp.where(is_last, 1, 0)
    down_slot = jnp.where(is_first, 0, 1)
    second = (k == 1, jnp.logical_not(is_last))
    half_width = x_ref.shape[1] // 2
    g_half = gram_local.shape[0] // 2
    g_part = g_half // z_devices
    c_half = cross_local.shape[0] // 2
    c_part = c_half // z_devices
    z_half_devices = z_devices // 2
    z_side = z // z_half_devices
    far_first = sorted(range(1, z_devices), key=lambda t: -min(t, z_devices - t))

    def peer(blk, t, other=False):
        return {"blk": blk, "row": lax.rem(z + t, z_devices) * 2 + (1 - core if other else core)}

    sibling = peer(k, 0, True)

    def remote(src, dst, send, recv, device):
        return pltpu.make_async_remote_copy(
            src_ref=src, dst_ref=dst, send_sem=send, recv_sem=recv,
            device_id=device, device_id_type=MESH,
        )

    def wait_for(ref, sem):
        pltpu.make_async_copy(ref, ref, sem).wait()

    def rows_at(start, size):
        return pl.ds(pl.multiple_of(start, 8), size)

    def either(condition, yes, no):
        pl.when(condition)(lambda: yes() and None)
        pl.when(jnp.logical_not(condition))(lambda: no() and None)

    def signal(sem, device):
        pl.semaphore_signal(sem, inc=1, device_id=device, device_id_type=MESH)

    load = pltpu.make_async_copy(x_hbm, x_ref, load_sem)
    load.start()

    barrier = pltpu.get_barrier_semaphore()
    for t in range(z_devices - 1, 0, -1):
        pl.when(z + t < z_devices)(functools.partial(signal, barrier, peer(k, t)))
    for edge, blk in ((is_last, up), (is_first, down)):
        for other in (False, True):
            pl.when(jnp.logical_not(edge))(functools.partial(signal, barrier, peer(blk, 0, other)))
    signal(barrier, sibling)

    load.wait()
    x_split = split(x_ref[...])
    g = dot3(x_split, x_split, 0)
    gram_local[:half_width] = g[:half_width, :half_width]
    gram_local[half_width : 2 * half_width] = g[:half_width, half_width:]
    gram_local[2 * half_width :] = g[half_width:, half_width:]

    neighbours = 2 - is_first.astype(jnp.int32) - is_last.astype(jnp.int32)
    pl.semaphore_wait(barrier, z + 1 + 2 * neighbours)
    for t in range(z_devices - 1, 0, -1):
        pl.when(z - t >= 0)(functools.partial(signal, here_sem, peer(k, z_devices - t)))

    gc = remote(gram_local.at[rows_at((1 - core) * g_half, g_half)], gram_core, gc_send, gc_recv, sibling)
    gc.start()

    x_up = remote(x_ref, moved.at[up_slot], x_send.at[0], x_recv.at[up_slot], peer(up, 0))
    x_down = remote(x_ref, moved.at[down_slot], x_send.at[1], x_recv.at[down_slot], peer(down, 0))
    either(is_last, pltpu.make_async_copy(x_ref, moved.at[1], x_recv.at[1]).start, x_up.start)
    either(is_first, pltpu.make_async_copy(x_ref, moved.at[0], x_recv.at[0]).start, x_down.start)

    def scatter(total, part, parts, send, recv):
        for t in far_first:
            there = rows_at(lax.rem(z + t, z_devices) * part, part)
            remote(total.at[there], parts.at[t - 1], send, recv, peer(k, t)).start()

    def gather(total, part, parts, recv):
        wait_for(parts, recv)
        terms = [total[rows_at(z * part, part)]] + [parts[n] for n in range(z_devices - 1)]
        while len(terms) > 1:
            terms = [a + b for a, b in zip(terms[::2], terms[1::2])]
        return terms[0]

    gc.wait_recv()
    gram_sum[...] = gram_local[rows_at(core * g_half, g_half)] + gram_core[...]

    @pl.when(z < z_devices - 1)
    def _():
        pl.semaphore_wait(here_sem, z_devices - 1 - z)

    scatter(gram_sum, g_part, gram_parts, gz_send, gz_recv)
    own_rows = rows_at(z * g_part, g_part)
    gram_full[own_rows] = gather(gram_sum, g_part, gram_parts, gz_recv)
    for t in far_first:
        remote(gram_full.at[own_rows], gram_full.at[own_rows], ga_send, ga_recv.at[z_side], peer(k, t)).start()

    for slot in range(2):
        wait_for(moved.at[slot], x_recv.at[slot])
    moved_split = [split(moved[slot]) for slot in range(2)]
    cross_local[...] = dot3(*moved_split, 0)
    cc = remote(cross_local.at[rows_at((1 - core) * c_half, c_half)], cross_core, cc_send, cc_recv, sibling)
    cc.start()
    cc.wait_recv()
    cross_sum[...] = cross_local[rows_at(core * c_half, c_half)] + cross_core[...]
    scatter(cross_sum, c_part, cross_parts, cz_send, cz_recv)

    side_rows = z_half_devices * g_part
    for side, count in ((z_side, z_half_devices - 1), (1 - z_side, z_half_devices)):
        wait_for(gram_full.at[pl.ds(0, count * g_part)], ga_recv.at[side])
        src = gram_full.at[rows_at(side * side_rows, side_rows)]
        there = rows_at(core * g_half + side * side_rows, side_rows)
        for n, (edge, blk, slot, own_slot) in enumerate(((is_last, up, up_slot, 1), (is_first, down, down_slot, 0))):
            dst = grams.at[slot, there]
            straight = remote(src, dst, straight_send.at[n], gx_recv.at[slot], peer(blk, 0))
            stays = pltpu.make_async_copy(src, grams.at[own_slot, there], gx_recv.at[own_slot])
            either(edge, stays.start, straight.start)
            remote(src, dst, across_send, gx_recv.at[slot], peer(blk, 0, True)).start()

    cross_shard[...] = gather(cross_sum, c_part, cross_parts, cz_recv)
    c_mine = rows_at(core * c_half + z * c_part, c_part)
    for t in far_first:
        remote(cross_shard, cross.at[c_mine], ca_send, ca_recv, peer(k, t)).start()
    pltpu.make_async_copy(cross_shard, cross.at[c_mine], ca_recv).start()

    for slot in range(2):
        wait_for(grams.at[slot], gx_recv.at[slot])
    diag_rows, roots_columns, scaled = [], [], []
    for slot in range(2):
        g = grams[slot]
        upper = g[half_width : 2 * half_width]
        full = jnp.concatenate(
            [
                jnp.concatenate([g[:half_width], upper], axis=1),
                jnp.concatenate([upper.T, g[2 * half_width :]], axis=1),
            ],
            axis=0,
        )
        column, line = diagonals(full)
        diag_rows.append(line)
        roots_columns.append(lax.rsqrt(column))
        scaled.append(full * roots_columns[slot] * lax.rsqrt(line))
    first = Solve(scaled)
    for _ in range(NSTEPS - 2):
        first.step()
    first.factors()
    zs, t_rows, its, ul = [], [], [], []
    for n in range(2):
        z_half = dot3(first.f[n], split(half_of(first.z[n], second[n], 1)))
        y_half = dot3(first.f[n], split(half_of(first.y[n], second[n], 1)))
        own = 4.0 * dot3(split(z_half), split(y_half), 0)
        t_column, t_row = diagonals(own)
        it_row = lax.rsqrt(t_row)
        t_rows.append(t_row)
        z_unit = z_half * it_row
        zs.append(split(z_unit))
        its.append(own * lax.rsqrt(t_column) * it_row)
        ul.append(split(dot3(moved_split[n], split(z_unit * roots_columns[n]))))
    ul = [jnp.concatenate([ul[0][p], ul[1][p]], axis=1) for p in range(2)]
    diag2 = jnp.concatenate([half_of(diag_rows[n], second[n], 1) * t_rows[n] for n in range(2)], axis=1)
    ends = math.sqrt(0.5) * jnp.sqrt(0.5 * diag2)
    root_row = lax.rsqrt(diag_rows[1])

    gc.wait_send()
    cc.wait_send()
    for parts, sem in ((gram_parts, gz_send), (gram_parts, ga_send), (cross_parts, cz_send), (cross_parts, ca_send)):
        wait_for(parts, sem)
    wait_for(grams.at[0], across_send)
    for n, (edge, copy) in enumerate(((is_last, x_up), (is_first, x_down))):

        @pl.when(jnp.logical_not(edge))
        def _(n=n, copy=copy):
            copy.wait_send()
            wait_for(gram_full, straight_send.at[n])

    here = cross.at[rows_at(core * c_half, c_half)]
    wait_for(here, ca_recv)
    cf = remote(here, here, cf_send, cf_recv, sibling)
    cf.start()
    cf.wait_recv()

    cross_scaled = cross[...] * roots_columns[0] * root_row
    off = dot3(zs[0], split(dot3(split(cross_scaled), zs[1])), 0)
    scaled2 = jnp.concatenate(
        [jnp.concatenate([its[0], off], axis=1), jnp.concatenate([off.T, its[1]], axis=1)], axis=0
    )
    last = Solve([scaled2])
    for _ in range(NSTEPS - 2):
        last.step()
    last.factors()
    almost = dot3(ul, last.z_split[0])
    out_ref[...] = dot3(split(almost), last.f[0]) * ends
    cf.wait_send()


def shards(blk_devices, z_devices, x):
    rows, width = x.shape
    half = width // 2
    dma = pltpu.SemaphoreType.DMA
    g_half, c_half = 3 * half // 2, width // 2
    others = z_devices - 1
    vmem = lambda *shape: pltpu.VMEM(shape, jnp.float32)
    return pl.pallas_call(
        functools.partial(kernel, blk_devices, z_devices),
        out_shape=jax.ShapeDtypeStruct(x.shape, jnp.float32),
        in_specs=[pl.BlockSpec(memory_space=pltpu.MemorySpace.HBM)],
        out_specs=pl.BlockSpec(memory_space=pltpu.VMEM),
        scratch_shapes=[
            vmem(rows, width), vmem(2, rows, width),
            vmem(3 * half, half), vmem(g_half, half), vmem(g_half, half),
            vmem(others, g_half // z_devices, half), vmem(g_half, half), vmem(2, 3 * half, half),
            vmem(width, width), vmem(c_half, width), vmem(c_half, width),
            vmem(others, c_half // z_devices, width), vmem(c_half // z_devices, width), vmem(width, width),
            pltpu.SemaphoreType.REGULAR, dma, dma((2,)), dma((2,)), dma, dma, dma, dma, dma, dma((2,)),
            dma((2,)), dma, dma((2,)), dma, dma, dma, dma, dma, dma, dma, dma,
        ],
        compiler_params=pltpu.CompilerParams(
            collective_id=0, has_side_effects=True, vmem_limit_bytes=32 * 1024 * 1024
        ),
        cost_estimate=pl.CostEstimate(
            flops=40 * 3 * 2 * width**3, bytes_accessed=8 * rows * width, transcendentals=4096
        ),
        name="rotate_pairs",
    )(pltpu.with_memory_space_constraint(x, pltpu.MemorySpace.HBM))


def solution(mesh):
    run = functools.partial(shards, mesh.shape["blk"], mesh.shape["row"] // 2)
    return jax.shard_map(
        run, mesh=mesh, in_specs=(P("row", "blk"),), out_specs=P("row", "blk"), check_vma=False
    )
```

```python
import functools
import math

import jax
import jax.numpy as jnp
from jax import lax
from jax.experimental import pallas as pl
from jax.experimental.pallas import tpu as pltpu
from jax.sharding import PartitionSpec as P

NSTEPS = 5
MESH = pl.DeviceIdType.MESH


def product(a, b, lhs_dim=1):
    return lax.dot_general(
        a, b, (((lhs_dim,), (0,)), ((), ())), preferred_element_type=jnp.float32
    )


def split(a):
    high = a.astype(jnp.bfloat16)
    return high, (a - high.astype(jnp.float32)).astype(jnp.bfloat16)


def dot3(a, b, lhs_dim=1):
    high, low = a
    if lhs_dim == 0:
        return product(high, b[0], 0) + (product(high, b[1], 0) + product(low, b[0], 0))
    half = high.shape[0] // 2
    blocks = []
    for rows in (slice(0, half), slice(half, 2 * half)):
        small = product(high[rows], b[1]) + product(low[rows], b[0])
        blocks.append(product(high[rows], b[0]) + small)
    return jnp.concatenate(blocks, axis=0)


def eye(n):
    rows = lax.broadcasted_iota(jnp.int32, (n, n), 0)
    columns = lax.broadcasted_iota(jnp.int32, (n, n), 1)
    return rows == columns


def diagonals(a):
    kept = jnp.where(eye(a.shape[0]), a, 0.0)
    return jnp.sum(kept, axis=1, keepdims=True), jnp.sum(kept, axis=0, keepdims=True)


class Solve:
    def __init__(self, starts):
        self.eye = jnp.where(eye(starts[0].shape[0]), 1.5, 0.0)
        y = [0.25 * m for m in starts]
        self.z = [self.eye - m for m in y]
        self.f = self.z_split = [split(z) for z in self.z]
        self.y = [dot3(f, split(m)) for f, m in zip(self.f, y)]
        self.y_split = [split(m) for m in self.y]

    def factors(self):
        self.f = [split(self.eye - dot3(y, z)) for y, z in zip(self.y_split, self.z_split)]

    def step(self):
        self.factors()
        self.z = [dot3(f, z) for f, z in zip(self.f, self.z_split)]
        self.z_split = [split(z) for z in self.z]
        self.y = [dot3(f, y) for f, y in zip(self.f, self.y_split)]
        self.y_split = [split(y) for y in self.y]


def half_of(a, second, axis):
    n = a.shape[axis] // 2
    first = lax.slice_in_dim(a, 0, n, axis=axis)
    return jnp.where(second, lax.slice_in_dim(a, n, 2 * n, axis=axis), first)


def kernel(
    blk_devices, z_devices,
    x_hbm, out_ref,
    x_ref, moved, gram_local, gram_core, gram_sum, gram_parts, gram_full, grams,
    cross_local, cross_core, cross_sum, cross_parts, cross_shard, cross, mixed_local, mixed_core,
    here_sem, load_sem, x_send, x_recv, gc_send, gc_recv, gz_send, gz_recv, ga_send, ga_recv,
    straight_send, across_send, gx_recv, cc_send, cc_recv, cz_send, cz_recv, ca_send, ca_recv, cf_send, cf_recv,
):
    k = lax.axis_index("blk")
    row = lax.axis_index("row")
    z = row // 2
    core = row % 2
    is_first = k == 0
    is_last = k == blk_devices - 1
    up = jnp.minimum(k + 1, blk_devices - 1)
    down = jnp.maximum(k - 1, 0)
    up_slot = jnp.where(is_last, 1, 0)
    down_slot = jnp.where(is_first, 0, 1)
    second = (k == 1, jnp.logical_not(is_last))
    half_width = x_ref.shape[1] // 2
    g_half = gram_local.shape[0] // 2
    g_part = g_half // z_devices
    c_half = cross_local.shape[0]
    c_part = c_half // z_devices
    z_half_devices = z_devices // 2
    z_side = z // z_half_devices
    far_first = sorted(range(1, z_devices), key=lambda t: -min(t, z_devices - t))

    def peer(blk, t, other=False):
        return {"blk": blk, "row": lax.rem(z + t, z_devices) * 2 + (1 - core if other else core)}

    sibling = peer(k, 0, True)

    def remote(src, dst, send, recv, device):
        return pltpu.make_async_remote_copy(
            src_ref=src, dst_ref=dst, send_sem=send, recv_sem=recv,
            device_id=device, device_id_type=MESH,
        )

    def wait_for(ref, sem):
        pltpu.make_async_copy(ref, ref, sem).wait()

    def rows_at(start, size):
        return pl.ds(pl.multiple_of(start, 8), size)

    def either(condition, yes, no):
        pl.when(condition)(lambda: yes() and None)
        pl.when(jnp.logical_not(condition))(lambda: no() and None)

    def signal(sem, device):
        pl.semaphore_signal(sem, inc=1, device_id=device, device_id_type=MESH)

    load = pltpu.make_async_copy(x_hbm, x_ref, load_sem)
    load.start()

    barrier = pltpu.get_barrier_semaphore()
    for edge, blk in ((is_last, up), (is_first, down)):
        for other in (False, True):
            pl.when(jnp.logical_not(edge))(functools.partial(signal, barrier, peer(blk, 0, other)))
    signal(barrier, sibling)
    for t in range(z_devices - 1, 0, -1):
        pl.when(z + t < z_devices)(functools.partial(signal, barrier, peer(k, t)))
    neighbours = 2 - is_first.astype(jnp.int32) - is_last.astype(jnp.int32)
    load.wait()
    pl.semaphore_wait(barrier, z + 1 + 2 * neighbours)

    x_up = remote(x_ref, moved.at[up_slot], x_send.at[0], x_recv.at[up_slot], peer(up, 0))
    x_down = remote(x_ref, moved.at[down_slot], x_send.at[1], x_recv.at[down_slot], peer(down, 0))
    either(is_last, pltpu.make_async_copy(x_ref, moved.at[1], x_recv.at[1]).start, x_up.start)
    either(is_first, pltpu.make_async_copy(x_ref, moved.at[0], x_recv.at[0]).start, x_down.start)

    for t in range(z_devices - 1, 0, -1):
        pl.when(z - t >= 0)(functools.partial(signal, here_sem.at[t - 1], peer(k, z_devices - t)))

    x_split = split(x_ref[...])
    g = dot3(x_split, x_split, 0)
    gram_local[:half_width] = g[:half_width, :half_width]
    gram_local[half_width : 2 * half_width] = g[:half_width, half_width:]
    gram_local[2 * half_width :] = g[half_width:, half_width:]

    gc = remote(gram_local.at[rows_at((1 - core) * g_half, g_half)], gram_core, gc_send, gc_recv, sibling)
    gc.start()

    def to_others(src, dst, send, recv):
        for there in range(z_devices):
            copy = remote(src, dst, send, recv, {"blk": k, "row": there * 2 + core})
            pl.when(z != there)(copy.start)

    def gather(total, part, parts, recv):
        wait_for(parts, recv)
        terms = [total[rows_at(z * part, part)]] + [parts[n] for n in range(z_devices - 1)]
        while len(terms) > 1:
            terms = [a + b for a, b in zip(terms[::2], terms[1::2])]
        return terms[0]

    gc.wait_recv()
    gram_sum[...] = gram_local[rows_at(core * g_half, g_half)] + gram_core[...]
    for owner in sorted(range(z_devices), key=lambda n: -min(n, z_devices - n)):

        @pl.when(z < owner)
        def _(owner=owner):
            pl.semaphore_wait(here_sem.at[owner - z - 1], 1)

        t = lax.rem(owner - z + z_devices, z_devices)
        copy = remote(
            gram_sum.at[pl.ds(owner * g_part, g_part)], gram_parts.at[t - 1], gz_send, gz_recv,
            {"blk": k, "row": owner * 2 + core},
        )
        pl.when(z != owner)(copy.start)

    own_rows = rows_at(z * g_part, g_part)

    gram_full[own_rows] = gather(gram_sum, g_part, gram_parts, gz_recv)
    to_others(gram_full.at[own_rows], gram_full.at[own_rows], ga_send, ga_recv.at[z_side])

    for slot in range(2):
        wait_for(moved.at[slot], x_recv.at[slot])
    b_split = split(moved[1])
    a_half = [half_of(moved[0], core == which, 1) for which in (0, 1)]
    cross_local[...] = dot3(split(a_half[0]), b_split, 0)
    cc = remote(cross_local, cross_core, cc_send, cc_recv, sibling)
    cc.start()
    cross_sum[...] = dot3(split(a_half[1]), b_split, 0)
    cc.wait_recv()
    cross_sum[...] += cross_core[...]
    for t in far_first:
        there = rows_at(lax.rem(z + t, z_devices) * c_part, c_part)
        remote(cross_sum.at[there], cross_parts.at[t - 1], cz_send, cz_recv, peer(k, t)).start()

    side_rows = z_half_devices * g_part
    for side, count in ((z_side, z_half_devices - 1), (1 - z_side, z_half_devices)):
        wait_for(gram_full.at[pl.ds(0, count * g_part)], ga_recv.at[side])
        src = gram_full.at[rows_at(side * side_rows, side_rows)]
        there = rows_at(core * g_half + side * side_rows, side_rows)
        for n, (edge, blk, slot, own_slot) in enumerate(((is_last, up, up_slot, 1), (is_first, down, down_slot, 0))):
            dst = grams.at[slot, there]
            straight = remote(src, dst, straight_send.at[n], gx_recv.at[slot], peer(blk, 0))
            stays = pltpu.make_async_copy(src, grams.at[own_slot, there], gx_recv.at[own_slot])
            either(edge, stays.start, straight.start)
            remote(src, dst, across_send, gx_recv.at[slot], peer(blk, 0, True)).start()

    cross_shard[...] = gather(cross_sum, c_part, cross_parts, cz_recv)
    c_mine = rows_at(z * c_part, c_part)
    to_others(cross_shard, cross.at[c_mine], ca_send, ca_recv)
    pltpu.make_async_copy(cross_shard, cross.at[c_mine], ca_recv).start()

    for slot in range(2):
        wait_for(grams.at[slot], gx_recv.at[slot])
    diag_rows, roots_columns, scaled = [], [], []
    for slot in range(2):
        g = grams[slot]
        upper = g[half_width : 2 * half_width]
        full = jnp.concatenate(
            [
                jnp.concatenate([g[:half_width], upper], axis=1),
                jnp.concatenate([upper.T, g[2 * half_width :]], axis=1),
            ],
            axis=0,
        )
        column, line = diagonals(full)
        diag_rows.append(line)
        roots_columns.append(lax.rsqrt(column))
        scaled.append(full * roots_columns[slot] * lax.rsqrt(line))
    first = Solve(scaled)
    for _ in range(NSTEPS - 2):
        first.step()
    first.factors()
    zs, t_rows, its, ul = [], [], [], []
    moved_split = [split(moved[slot]) for slot in range(2)]
    for n in range(2):
        z_half = dot3(first.f[n], split(half_of(first.z[n], second[n], 1)))
        y_half = dot3(first.f[n], split(half_of(first.y[n], second[n], 1)))
        own = 4.0 * dot3(split(z_half), split(y_half), 0)
        t_column, t_row = diagonals(own)
        it_row = lax.rsqrt(t_row)
        t_rows.append(t_row)
        z_unit = z_half * it_row
        zs.append(z_unit)
        its.append(own * lax.rsqrt(t_column) * it_row)
        ul.append(split(z_unit * roots_columns[n]))
    diag2 = jnp.concatenate([half_of(diag_rows[n], second[n], 1) * t_rows[n] for n in range(2)], axis=1)
    ends = math.sqrt(0.5) * jnp.sqrt(0.5 * diag2)
    root_row = lax.rsqrt(diag_rows[1])

    gc.wait_send()
    cc.wait_send()
    for parts, sem in ((gram_parts, gz_send), (gram_parts, ga_send), (cross_parts, cz_send), (cross_parts, ca_send)):
        wait_for(parts, sem)
    wait_for(grams.at[0], across_send)
    for n, (edge, copy) in enumerate(((is_last, x_up), (is_first, x_down))):

        @pl.when(jnp.logical_not(edge))
        def _(n=n, copy=copy):
            copy.wait_send()
            wait_for(gram_full, straight_send.at[n])

    z_rows = split(half_of(zs[0], core == 1, 0))
    z_other = split(zs[1])
    roots_half = half_of(roots_columns[0], core == 1, 0)
    wait_for(cross, ca_recv)
    turned = dot3(split(cross[...] * roots_half * root_row), z_other)
    mixed_local[...] = dot3(z_rows, split(turned), 0)
    cf = remote(mixed_local, mixed_core, cf_send, cf_recv, sibling)
    cf.start()
    cf.wait_recv()
    off = mixed_local[...] + mixed_core[...]
    scaled2 = jnp.concatenate(
        [jnp.concatenate([its[0], off], axis=1), jnp.concatenate([off.T, its[1]], axis=1)], axis=0
    )
    last = Solve([scaled2])
    last.step()
    ul = [split(dot3(moved_split[n], ul[n])) for n in range(2)]
    ul = [jnp.concatenate([ul[0][p], ul[1][p]], axis=1) for p in range(2)]
    for _ in range(NSTEPS - 3):
        last.step()
    last.factors()
    almost = dot3(ul, last.z_split[0])
    out_ref[...] = dot3(split(almost), last.f[0]) * ends
    cf.wait_send()


def shards(blk_devices, z_devices, x):
    rows, width = x.shape
    half = width // 2
    dma = pltpu.SemaphoreType.DMA
    g_half, c_half = 3 * half // 2, width // 2
    others = z_devices - 1
    vmem = lambda *shape: pltpu.VMEM(shape, jnp.float32)
    return pl.pallas_call(
        functools.partial(kernel, blk_devices, z_devices),
        out_shape=jax.ShapeDtypeStruct(x.shape, jnp.float32),
        in_specs=[pl.BlockSpec(memory_space=pltpu.MemorySpace.HBM)],
        out_specs=pl.BlockSpec(memory_space=pltpu.VMEM),
        scratch_shapes=[
            vmem(rows, width), vmem(2, rows, width),
            vmem(3 * half, half), vmem(g_half, half), vmem(g_half, half),
            vmem(others, g_half // z_devices, half), vmem(g_half, half), vmem(2, 3 * half, half),
            vmem(c_half, width), vmem(c_half, width), vmem(c_half, width),
            vmem(others, c_half // z_devices, width), vmem(c_half // z_devices, width), vmem(c_half, width),
            vmem(half, half), vmem(half, half),
            pltpu.SemaphoreType.REGULAR((others,)), dma, dma((2,)), dma((2,)), dma, dma, dma, dma, dma, dma((2,)),
            dma((2,)), dma, dma((2,)), dma, dma, dma, dma, dma, dma, dma, dma,
        ],
        compiler_params=pltpu.CompilerParams(
            collective_id=0, has_side_effects=True, vmem_limit_bytes=32 * 1024 * 1024
        ),
        cost_estimate=pl.CostEstimate(
            flops=40 * 3 * 2 * width**3, bytes_accessed=8 * rows * width, transcendentals=4096
        ),
        name="rotate_pairs",
    )(pltpu.with_memory_space_constraint(x, pltpu.MemorySpace.HBM))


def solution(mesh):
    run = functools.partial(shards, mesh.shape["blk"], mesh.shape["row"] // 2)
    return jax.shard_map(
        run, mesh=mesh, in_specs=(P("row", "blk"),), out_specs=P("row", "blk"), check_vma=False
    )
```

```python
import functools
import math

import jax
import jax.numpy as jnp
from jax import lax
from jax.experimental import pallas as pl
from jax.experimental.pallas import tpu as pltpu
from jax.sharding import PartitionSpec as P

NSTEPS = 5
MESH = pl.DeviceIdType.MESH


def product(a, b, lhs_dim=1):
    return lax.dot_general(
        a, b, (((lhs_dim,), (0,)), ((), ())), preferred_element_type=jnp.float32
    )


def split(a):
    high = a.astype(jnp.bfloat16)
    return high, (a - high.astype(jnp.float32)).astype(jnp.bfloat16)


def dot3(a, b, lhs_dim=1):
    high, low = a
    if lhs_dim == 0:
        return product(high, b[0], 0) + (product(high, b[1], 0) + product(low, b[0], 0))
    half = high.shape[0] // 2
    blocks = []
    for rows in (slice(0, half), slice(half, 2 * half)):
        small = product(high[rows], b[1]) + product(low[rows], b[0])
        blocks.append(product(high[rows], b[0]) + small)
    return jnp.concatenate(blocks, axis=0)


def eye(n):
    rows = lax.broadcasted_iota(jnp.int32, (n, n), 0)
    columns = lax.broadcasted_iota(jnp.int32, (n, n), 1)
    return rows == columns


def diagonals(a):
    kept = jnp.where(eye(a.shape[0]), a, 0.0)
    return jnp.sum(kept, axis=1, keepdims=True), jnp.sum(kept, axis=0, keepdims=True)


class Solve:
    def __init__(self, starts):
        self.eye = jnp.where(eye(starts[0].shape[0]), 1.5, 0.0)
        y = [0.25 * m for m in starts]
        self.z = [self.eye - m for m in y]
        self.f = self.z_split = [split(z) for z in self.z]
        self.y = [dot3(f, split(m)) for f, m in zip(self.f, y)]
        self.y_split = [split(m) for m in self.y]

    def factors(self):
        self.f = [split(self.eye - dot3(y, z)) for y, z in zip(self.y_split, self.z_split)]

    def step(self):
        self.factors()
        self.z = [dot3(f, z) for f, z in zip(self.f, self.z_split)]
        self.z_split = [split(z) for z in self.z]
        self.y = [dot3(f, y) for f, y in zip(self.f, self.y_split)]
        self.y_split = [split(y) for y in self.y]


def half_of(a, second, axis):
    n = a.shape[axis] // 2
    first = lax.slice_in_dim(a, 0, n, axis=axis)
    return jnp.where(second, lax.slice_in_dim(a, n, 2 * n, axis=axis), first)


def kernel(
    blk_devices, z_devices,
    x_hbm, out_ref,
    x_ref, moved, gram_local, gram_core, gram_sum, gram_parts, gram_shard, gram_full, grams,
    cross_local, cross_core, cross_sum, cross_parts, cross_shard, cross, mixed_local, mixed_core,
    here_sem, load_sem, x_send, x_recv, gc_send, gc_recv, gz_send, gz_recv, ga_send, ga_recv,
    straight_send, across_send, gx_recv, cc_send, cc_recv, cz_send, cz_recv, ca_send, ca_recv, cf_send, cf_recv,
):
    k = lax.axis_index("blk")
    row = lax.axis_index("row")
    z = row // 2
    core = row % 2
    is_first = k == 0
    is_last = k == blk_devices - 1
    up = jnp.minimum(k + 1, blk_devices - 1)
    down = jnp.maximum(k - 1, 0)
    up_slot = jnp.where(is_last, 1, 0)
    down_slot = jnp.where(is_first, 0, 1)
    second = (k == 1, jnp.logical_not(is_last))
    half_width = x_ref.shape[1] // 2
    g_half = gram_local.shape[0] // 2
    g_part = half_width // z_devices
    g_parts = [(0, g_part + 8)] + [(8 + n * g_part, g_part) for n in range(1, z_devices)]
    c_half = cross_local.shape[0]
    c_part = c_half // z_devices
    middle = z_devices // 2
    lower_side = z < middle
    far_first = sorted(range(1, z_devices), key=lambda t: -min(t, z_devices - t))

    def peer(blk, t, other=False):
        return {"blk": blk, "row": lax.rem(z + t, z_devices) * 2 + (1 - core if other else core)}

    sibling = peer(k, 0, True)

    def remote(src, dst, send, recv, device):
        return pltpu.make_async_remote_copy(
            src_ref=src, dst_ref=dst, send_sem=send, recv_sem=recv,
            device_id=device, device_id_type=MESH,
        )

    def wait_for(ref, sem):
        pltpu.make_async_copy(ref, ref, sem).wait()

    def rows_at(start, size):
        return pl.ds(pl.multiple_of(start, 8), size)

    def either(condition, yes, no):
        pl.when(condition)(lambda: yes() and None)
        pl.when(jnp.logical_not(condition))(lambda: no() and None)

    def signal(sem, device):
        pl.semaphore_signal(sem, inc=1, device_id=device, device_id_type=MESH)

    load = pltpu.make_async_copy(x_hbm, x_ref, load_sem)
    load.start()

    barrier = pltpu.get_barrier_semaphore()
    for edge, blk in ((is_last, up), (is_first, down)):
        for other in (False, True):
            pl.when(jnp.logical_not(edge))(functools.partial(signal, barrier, peer(blk, 0, other)))
    signal(barrier, sibling)
    for t in range(z_devices - 1, 0, -1):
        pl.when(z + t < z_devices)(functools.partial(signal, barrier, peer(k, t)))
    neighbours = 2 - is_first.astype(jnp.int32) - is_last.astype(jnp.int32)
    load.wait()
    pl.semaphore_wait(barrier, z + 1 + 2 * neighbours)

    x_up = remote(x_ref, moved.at[up_slot], x_send.at[0], x_recv.at[up_slot], peer(up, 0))
    x_down = remote(x_ref, moved.at[down_slot], x_send.at[1], x_recv.at[down_slot], peer(down, 0))
    either(is_last, pltpu.make_async_copy(x_ref, moved.at[1], x_recv.at[1]).start, x_up.start)
    either(is_first, pltpu.make_async_copy(x_ref, moved.at[0], x_recv.at[0]).start, x_down.start)

    for t in range(z_devices - 1, 0, -1):
        pl.when(z - t >= 0)(functools.partial(signal, here_sem.at[t - 1], peer(k, z_devices - t)))

    x_split = split(x_ref[...])
    g = dot3(x_split, x_split, 0)
    block_rows = lax.broadcasted_iota(jnp.int32, (half_width, half_width), 0)
    block_columns = lax.broadcasted_iota(jnp.int32, (half_width, half_width), 1)
    gram_local[:half_width] = g[:half_width, half_width:]
    gram_local[half_width:g_half] = jnp.zeros((8, half_width), jnp.float32)
    gram_local[g_half : g_half + half_width] = jnp.where(
        block_rows >= block_columns, g[:half_width, :half_width], g[half_width:, half_width:]
    )
    gram_local[g_half + half_width :] = jnp.broadcast_to(diagonals(g[half_width:, half_width:])[1], (8, half_width))

    gc = remote(gram_local.at[rows_at((1 - core) * g_half, g_half)], gram_core, gc_send, gc_recv, sibling)
    gc.start()

    def to_others(src, dst, send, recv):
        for there in range(z_devices):
            copy = remote(src, dst, send, recv, {"blk": k, "row": there * 2 + core})
            pl.when(z != there)(copy.start)

    def tree(terms):
        while len(terms) > 1:
            terms = [a + b for a, b in zip(terms[::2], terms[1::2])]
        return terms[0]

    gc.wait_recv()
    gram_sum[...] = gram_local[rows_at(core * g_half, g_half)] + gram_core[...]
    for owner in sorted(range(z_devices), key=lambda n: -min(n, z_devices - n)):

        @pl.when(z < owner)
        def _(owner=owner):
            pl.semaphore_wait(here_sem.at[owner - z - 1], 1)

        t = lax.rem(owner - z + z_devices, z_devices)
        start, size = g_parts[owner]
        copy = remote(
            gram_sum.at[pl.ds(start, size)], gram_parts.at[jnp.maximum(t - 1, 0), pl.ds(0, size)], gz_send, gz_recv,
            {"blk": k, "row": owner * 2 + core},
        )
        pl.when(z != owner)(copy.start)

    def own_part(start, size):
        wait_for(grams.at[0, pl.ds(0, (z_devices - 1) * size)], gz_recv)
        gram_shard[:size] = tree(
            [gram_sum[pl.ds(start, size)]] + [gram_parts[n, :size] for n in range(z_devices - 1)]
        )
        src, dst = gram_shard.at[pl.ds(0, size)], gram_full.at[pl.ds(start, size)]
        sem = ga_recv.at[jnp.where(lower_side, 0, 1)]
        pltpu.make_async_copy(src, dst, sem).start()
        to_others(src, dst, ga_send, sem)

    either(
        z == 0,
        functools.partial(own_part, *g_parts[0]),
        lambda: own_part(pl.multiple_of(8 + z * g_part, 8), g_part),
    )

    for slot in range(2):
        wait_for(moved.at[slot], x_recv.at[slot])
    b_split = split(moved[1])
    a_half = [half_of(moved[0], core == which, 1) for which in (0, 1)]
    cross_local[...] = dot3(split(a_half[0]), b_split, 0)
    cc = remote(cross_local, cross_core, cc_send, cc_recv, sibling)
    cc.start()
    cross_sum[...] = dot3(split(a_half[1]), b_split, 0)
    cc.wait_recv()
    cross_sum[...] += cross_core[...]
    for t in far_first:
        there = rows_at(lax.rem(z + t, z_devices) * c_part, c_part)
        remote(cross_sum.at[there], cross_parts.at[t - 1], cz_send, cz_recv, peer(k, t)).start()

    def forward(side):
        start = g_parts[side * middle][0]
        size = (g_parts[middle][0], g_half - g_parts[middle][0])[side]
        src = gram_full.at[pl.ds(start, size)]
        there = rows_at(core * g_half + start, size)
        wait_for(src, ga_recv.at[side])
        for n, (edge, blk, slot, own_slot) in enumerate(((is_last, up, up_slot, 1), (is_first, down, down_slot, 0))):
            dst = grams.at[slot, there]
            straight = remote(src, dst, straight_send.at[n], gx_recv.at[slot], peer(blk, 0))
            stays = pltpu.make_async_copy(src, grams.at[own_slot, there], gx_recv.at[own_slot])
            either(edge, stays.start, straight.start)
            remote(src, dst, across_send, gx_recv.at[slot], peer(blk, 0, True)).start()

    either(lower_side, lambda: (forward(0), forward(1)), lambda: (forward(1), forward(0)))

    wait_for(cross_parts, cz_recv)
    cross_shard[...] = tree([cross_sum[rows_at(z * c_part, c_part)]] + [cross_parts[n] for n in range(z_devices - 1)])
    c_mine = rows_at(z * c_part, c_part)
    to_others(cross_shard, cross.at[c_mine], ca_send, ca_recv)
    pltpu.make_async_copy(cross_shard, cross.at[c_mine], ca_recv).start()

    for slot in range(2):
        wait_for(grams.at[slot], gx_recv.at[slot])
    diag_rows, roots_columns, scaled = [], [], []
    for slot in range(2):
        upper = grams[slot, pl.ds(0, half_width)]
        packed = grams[slot, pl.ds(g_half, half_width)]
        corner = jnp.where(block_rows < block_columns, packed, packed.T)
        corner = jnp.where(block_rows == block_columns, grams[slot, pl.ds(g_half + half_width, 1)], corner)
        full = jnp.concatenate(
            [
                jnp.concatenate([jnp.where(block_rows >= block_columns, packed, packed.T), upper], axis=1),
                jnp.concatenate([upper.T, corner], axis=1),
            ],
            axis=0,
        )
        column, line = diagonals(full)
        diag_rows.append(line)
        roots_columns.append(lax.rsqrt(column))
        scaled.append(full * roots_columns[slot] * lax.rsqrt(line))
    first = Solve(scaled)
    for _ in range(NSTEPS - 2):
        first.step()
    first.factors()
    zs, t_rows, its, ul = [], [], [], []
    moved_split = [split(moved[slot]) for slot in range(2)]
    for n in range(2):
        z_half = dot3(first.f[n], split(half_of(first.z[n], second[n], 1)))
        y_half = dot3(first.f[n], split(half_of(first.y[n], second[n], 1)))
        own = 4.0 * dot3(split(z_half), split(y_half), 0)
        t_column, t_row = diagonals(own)
        it_row = lax.rsqrt(t_row)
        t_rows.append(t_row)
        z_unit = z_half * it_row
        zs.append(z_unit)
        its.append(own * lax.rsqrt(t_column) * it_row)
        ul.append(split(z_unit * roots_columns[n]))
    diag2 = jnp.concatenate([half_of(diag_rows[n], second[n], 1) * t_rows[n] for n in range(2)], axis=1)
    ends = math.sqrt(0.5) * jnp.sqrt(0.5 * diag2)
    root_row = lax.rsqrt(diag_rows[1])

    gc.wait_send()
    cc.wait_send()
    wait_for(cross_parts, cz_send)
    wait_for(cross_parts, ca_send)

    def own_sent(gz_rows, ga_rows):
        wait_for(grams.at[0, pl.ds(0, gz_rows)], gz_send)
        wait_for(grams.at[0, pl.ds(0, ga_rows)], ga_send)

    others = z_devices - 1
    either(
        z == 0,
        lambda: own_sent(others * g_part, others * (g_part + 8)),
        lambda: own_sent(others * g_part + 8, others * g_part),
    )
    wait_for(grams.at[0], across_send)
    for n, (edge, copy) in enumerate(((is_last, x_up), (is_first, x_down))):

        @pl.when(jnp.logical_not(edge))
        def _(n=n, copy=copy):
            copy.wait_send()
            wait_for(gram_full, straight_send.at[n])

    z_rows = split(half_of(zs[0], core == 1, 0))
    z_other = split(zs[1])
    roots_half = half_of(roots_columns[0], core == 1, 0)
    wait_for(cross, ca_recv)
    turned = dot3(split(cross[...] * roots_half * root_row), z_other)
    mixed_local[...] = dot3(z_rows, split(turned), 0)
    cf = remote(mixed_local, mixed_core, cf_send, cf_recv, sibling)
    cf.start()
    cf.wait_recv()
    off = mixed_local[...] + mixed_core[...]
    scaled2 = jnp.concatenate(
        [jnp.concatenate([its[0], off], axis=1), jnp.concatenate([off.T, its[1]], axis=1)], axis=0
    )
    last = Solve([scaled2])
    last.step()
    ul = [split(dot3(moved_split[n], ul[n])) for n in range(2)]
    ul = [jnp.concatenate([ul[0][p], ul[1][p]], axis=1) for p in range(2)]
    for _ in range(NSTEPS - 3):
        last.step()
    last.factors()
    almost = dot3(ul, last.z_split[0])
    out_ref[...] = dot3(split(almost), last.f[0]) * ends
    cf.wait_send()


def shards(blk_devices, z_devices, x):
    rows, width = x.shape
    half = width // 2
    dma = pltpu.SemaphoreType.DMA
    g_half, c_half = half + 8, width // 2
    g_part = half // z_devices + 8
    others = z_devices - 1
    vmem = lambda *shape: pltpu.VMEM(shape, jnp.float32)
    return pl.pallas_call(
        functools.partial(kernel, blk_devices, z_devices),
        out_shape=jax.ShapeDtypeStruct(x.shape, jnp.float32),
        in_specs=[pl.BlockSpec(memory_space=pltpu.MemorySpace.HBM)],
        out_specs=pl.BlockSpec(memory_space=pltpu.VMEM),
        scratch_shapes=[
            vmem(rows, width), vmem(2, rows, width),
            vmem(2 * g_half, half), vmem(g_half, half), vmem(g_half, half),
            vmem(others, g_part, half), vmem(g_part, half), vmem(g_half, half), vmem(2, 2 * g_half, half),
            vmem(c_half, width), vmem(c_half, width), vmem(c_half, width),
            vmem(others, c_half // z_devices, width), vmem(c_half // z_devices, width), vmem(c_half, width),
            vmem(half, half), vmem(half, half),
            pltpu.SemaphoreType.REGULAR((others,)), dma, dma((2,)), dma((2,)), dma, dma, dma, dma, dma, dma((2,)),
            dma((2,)), dma, dma((2,)), dma, dma, dma, dma, dma, dma, dma, dma,
        ],
        compiler_params=pltpu.CompilerParams(
            collective_id=0, has_side_effects=True, vmem_limit_bytes=32 * 1024 * 1024
        ),
        cost_estimate=pl.CostEstimate(
            flops=40 * 3 * 2 * width**3, bytes_accessed=8 * rows * width, transcendentals=4096
        ),
        name="rotate_pairs",
    )(pltpu.with_memory_space_constraint(x, pltpu.MemorySpace.HBM))


def solution(mesh):
    run = functools.partial(shards, mesh.shape["blk"], mesh.shape["row"] // 2)
    return jax.shard_map(
        run, mesh=mesh, in_specs=(P("row", "blk"),), out_specs=P("row", "blk"), check_vma=False
    )
```

```python
import functools
import math

import jax
import jax.numpy as jnp
from jax import lax
from jax.experimental import pallas as pl
from jax.experimental.pallas import tpu as pltpu
from jax.sharding import PartitionSpec as P

NSTEPS = 5
MESH = pl.DeviceIdType.MESH


def product(a, b, lhs_dim=1):
    return lax.dot_general(
        a, b, (((lhs_dim,), (0,)), ((), ())), preferred_element_type=jnp.float32
    )


def split(a):
    high = a.astype(jnp.bfloat16)
    return high, (a - high.astype(jnp.float32)).astype(jnp.bfloat16)


def dot3(a, b, lhs_dim=1):
    high, low = a
    if lhs_dim == 0:
        return product(high, b[0], 0) + (product(high, b[1], 0) + product(low, b[0], 0))
    half = high.shape[0] // 2
    blocks = []
    for rows in (slice(0, half), slice(half, 2 * half)):
        small = product(high[rows], b[1]) + product(low[rows], b[0])
        blocks.append(product(high[rows], b[0]) + small)
    return jnp.concatenate(blocks, axis=0)


def eye(n):
    rows = lax.broadcasted_iota(jnp.int32, (n, n), 0)
    columns = lax.broadcasted_iota(jnp.int32, (n, n), 1)
    return rows == columns


def diagonals(a):
    kept = jnp.where(eye(a.shape[0]), a, 0.0)
    return jnp.sum(kept, axis=1, keepdims=True), jnp.sum(kept, axis=0, keepdims=True)


class Solve:
    def __init__(self, starts):
        self.eye = jnp.where(eye(starts[0].shape[0]), 1.5, 0.0)
        y = [0.25 * m for m in starts]
        self.z = [self.eye - m for m in y]
        self.f = self.z_split = [split(z) for z in self.z]
        self.y = [dot3(f, split(m)) for f, m in zip(self.f, y)]
        self.y_split = [split(m) for m in self.y]

    def factors(self):
        self.f = [split(self.eye - dot3(y, z)) for y, z in zip(self.y_split, self.z_split)]

    def step(self):
        self.factors()
        self.z = [dot3(f, z) for f, z in zip(self.f, self.z_split)]
        self.z_split = [split(z) for z in self.z]
        self.y = [dot3(f, y) for f, y in zip(self.f, self.y_split)]
        self.y_split = [split(y) for y in self.y]


def half_of(a, second, axis):
    n = a.shape[axis] // 2
    first = lax.slice_in_dim(a, 0, n, axis=axis)
    return jnp.where(second, lax.slice_in_dim(a, n, 2 * n, axis=axis), first)


def kernel(
    blk_devices, z_devices,
    x_hbm, out_ref,
    x_ref, moved, gram_local, gram_core, gram_sum, gram_parts, gram_shard, gram_full, grams,
    cross_local, cross_core, cross_sum, cross_parts, cross_shard, cross, mixed_local, mixed_core,
    here_sem, load_sem, x_send, x_recv, gc_send, gc_recv, gz_send, gz_recv, ga_send, ga_recv,
    straight_send, across_send, gx_recv, cc_send, cc_recv, cz_send, cz_recv, ca_send, ca_recv, cf_send, cf_recv,
):
    k = lax.axis_index("blk")
    row = lax.axis_index("row")
    z = row // 2
    core = row % 2
    is_first = k == 0
    is_last = k == blk_devices - 1
    up = jnp.minimum(k + 1, blk_devices - 1)
    down = jnp.maximum(k - 1, 0)
    up_slot = jnp.where(is_last, 1, 0)
    down_slot = jnp.where(is_first, 0, 1)
    second = (k == 1, jnp.logical_not(is_last))
    half_width = x_ref.shape[1] // 2
    g_half = gram_local.shape[0] // 2
    g_part = half_width // z_devices
    g_parts = [(0, g_part + 8)] + [(8 + n * g_part, g_part) for n in range(1, z_devices)]
    c_half = cross_local.shape[0]
    c_part = c_half // z_devices
    middle = z_devices // 2
    lower_side = z < middle
    far_first = sorted(range(1, z_devices), key=lambda t: -min(t, z_devices - t))

    def peer(blk, t, other=False):
        return {"blk": blk, "row": lax.rem(z + t, z_devices) * 2 + (1 - core if other else core)}

    sibling = peer(k, 0, True)

    def remote(src, dst, send, recv, device):
        return pltpu.make_async_remote_copy(
            src_ref=src, dst_ref=dst, send_sem=send, recv_sem=recv,
            device_id=device, device_id_type=MESH,
        )

    def wait_for(ref, sem):
        pltpu.make_async_copy(ref, ref, sem).wait()

    def rows_at(start, size):
        return pl.ds(pl.multiple_of(start, 8), size)

    def either(condition, yes, no):
        pl.when(condition)(lambda: yes() and None)
        pl.when(jnp.logical_not(condition))(lambda: no() and None)

    def signal(sem, device):
        pl.semaphore_signal(sem, inc=1, device_id=device, device_id_type=MESH)

    load = pltpu.make_async_copy(x_hbm, x_ref, load_sem)
    load.start()

    barrier = pltpu.get_barrier_semaphore()
    for edge, blk in ((is_last, up), (is_first, down)):
        for other in (False, True):
            pl.when(jnp.logical_not(edge))(functools.partial(signal, barrier, peer(blk, 0, other)))
    signal(barrier, sibling)
    for t in range(z_devices - 1, 0, -1):
        pl.when(z + t < z_devices)(functools.partial(signal, barrier, peer(k, t)))
    neighbours = 2 - is_first.astype(jnp.int32) - is_last.astype(jnp.int32)

    load.wait()
    x_split = split(x_ref[...])
    g = dot3(x_split, x_split, 0)
    block_rows = lax.broadcasted_iota(jnp.int32, (half_width, half_width), 0)
    block_columns = lax.broadcasted_iota(jnp.int32, (half_width, half_width), 1)
    gram_local[:half_width] = g[:half_width, half_width:]
    gram_local[half_width:g_half] = jnp.zeros((8, half_width), jnp.float32)
    gram_local[g_half : g_half + half_width] = jnp.where(
        block_rows >= block_columns, g[:half_width, :half_width], g[half_width:, half_width:]
    )
    gram_local[g_half + half_width :] = jnp.broadcast_to(diagonals(g[half_width:, half_width:])[1], (8, half_width))

    pl.semaphore_wait(barrier, z + 1 + 2 * neighbours)

    for t in range(z_devices - 1, 0, -1):
        pl.when(z - t >= 0)(functools.partial(signal, here_sem.at[t - 1], peer(k, z_devices - t)))

    gc = remote(gram_local.at[rows_at((1 - core) * g_half, g_half)], gram_core, gc_send, gc_recv, sibling)
    gc.start()

    x_up = remote(x_ref, moved.at[up_slot], x_send.at[0], x_recv.at[up_slot], peer(up, 0))
    x_down = remote(x_ref, moved.at[down_slot], x_send.at[1], x_recv.at[down_slot], peer(down, 0))
    either(is_last, pltpu.make_async_copy(x_ref, moved.at[1], x_recv.at[1]).start, x_up.start)
    either(is_first, pltpu.make_async_copy(x_ref, moved.at[0], x_recv.at[0]).start, x_down.start)


    def to_others(src, dst, send, recv):
        for there in range(z_devices):
            copy = remote(src, dst, send, recv, {"blk": k, "row": there * 2 + core})
            pl.when(z != there)(copy.start)

    def tree(terms):
        while len(terms) > 1:
            terms = [a + b for a, b in zip(terms[::2], terms[1::2])]
        return terms[0]

    gc.wait_recv()
    gram_sum[...] = gram_local[rows_at(core * g_half, g_half)] + gram_core[...]
    for owner in sorted(range(z_devices), key=lambda n: -min(n, z_devices - n)):

        @pl.when(z < owner)
        def _(owner=owner):
            pl.semaphore_wait(here_sem.at[owner - z - 1], 1)

        t = lax.rem(owner - z + z_devices, z_devices)
        start, size = g_parts[owner]
        copy = remote(
            gram_sum.at[pl.ds(start, size)], gram_parts.at[jnp.maximum(t - 1, 0), pl.ds(0, size)], gz_send, gz_recv,
            {"blk": k, "row": owner * 2 + core},
        )
        pl.when(z != owner)(copy.start)

    def own_part(start, size):
        wait_for(grams.at[0, pl.ds(0, (z_devices - 1) * size)], gz_recv)
        gram_shard[:size] = tree(
            [gram_sum[pl.ds(start, size)]] + [gram_parts[n, :size] for n in range(z_devices - 1)]
        )
        src, dst = gram_shard.at[pl.ds(0, size)], gram_full.at[pl.ds(start, size)]
        sem = ga_recv.at[jnp.where(lower_side, 0, 1)]
        pltpu.make_async_copy(src, dst, sem).start()
        to_others(src, dst, ga_send, sem)

    cc = remote(cross_local, cross_core, cc_send, cc_recv, sibling)

    def gram_sum_part():
        either(
            z == 0,
            functools.partial(own_part, *g_parts[0]),
            lambda: own_part(pl.multiple_of(8 + z * g_part, 8), g_part),
        )

    def cross_part():
        for slot in range(2):
            wait_for(moved.at[slot], x_recv.at[slot])
        b_split = split(moved[1])
        a_half = [half_of(moved[0], core == which, 1) for which in (0, 1)]
        cross_local[...] = dot3(split(a_half[0]), b_split, 0)
        cc.start()
        cross_sum[...] = dot3(split(a_half[1]), b_split, 0)
    either(
        lower_side,
        lambda: (cross_part(), gram_sum_part()),
        lambda: (gram_sum_part(), cross_part()),
    )

    cc.wait_recv()
    cross_sum[...] += cross_core[...]
    for t in far_first:
        there = rows_at(lax.rem(z + t, z_devices) * c_part, c_part)
        remote(cross_sum.at[there], cross_parts.at[t - 1], cz_send, cz_recv, peer(k, t)).start()

    def forward(side):
        start = g_parts[side * middle][0]
        size = (g_parts[middle][0], g_half - g_parts[middle][0])[side]
        src = gram_full.at[pl.ds(start, size)]
        there = rows_at(core * g_half + start, size)
        wait_for(src, ga_recv.at[side])
        for n, (edge, blk, slot, own_slot) in enumerate(((is_last, up, up_slot, 1), (is_first, down, down_slot, 0))):
            dst = grams.at[slot, there]
            straight = remote(src, dst, straight_send.at[n], gx_recv.at[slot], peer(blk, 0))
            stays = pltpu.make_async_copy(src, grams.at[own_slot, there], gx_recv.at[own_slot])
            either(edge, stays.start, straight.start)
            remote(src, dst, across_send, gx_recv.at[slot], peer(blk, 0, True)).start()

    either(lower_side, lambda: (forward(0), forward(1)), lambda: (forward(1), forward(0)))

    wait_for(cross_parts, cz_recv)
    cross_shard[...] = tree([cross_sum[rows_at(z * c_part, c_part)]] + [cross_parts[n] for n in range(z_devices - 1)])
    c_mine = rows_at(z * c_part, c_part)
    to_others(cross_shard, cross.at[c_mine], ca_send, ca_recv)
    pltpu.make_async_copy(cross_shard, cross.at[c_mine], ca_recv).start()

    for slot in range(2):
        wait_for(grams.at[slot], gx_recv.at[slot])
    diag_rows, roots_columns, scaled = [], [], []
    for slot in range(2):
        upper = grams[slot, pl.ds(0, half_width)]
        packed = grams[slot, pl.ds(g_half, half_width)]
        corner = jnp.where(block_rows < block_columns, packed, packed.T)
        corner = jnp.where(block_rows == block_columns, grams[slot, pl.ds(g_half + half_width, 1)], corner)
        full = jnp.concatenate(
            [
                jnp.concatenate([jnp.where(block_rows >= block_columns, packed, packed.T), upper], axis=1),
                jnp.concatenate([upper.T, corner], axis=1),
            ],
            axis=0,
        )
        column, line = diagonals(full)
        diag_rows.append(line)
        roots_columns.append(lax.rsqrt(column))
        scaled.append(full * roots_columns[slot] * lax.rsqrt(line))
    first = Solve(scaled)
    for _ in range(NSTEPS - 2):
        first.step()
    first.factors()
    zs, t_rows, its, ul = [], [], [], []
    moved_split = [split(moved[slot]) for slot in range(2)]
    for n in range(2):
        z_half = dot3(first.f[n], split(half_of(first.z[n], second[n], 1)))
        y_half = dot3(first.f[n], split(half_of(first.y[n], second[n], 1)))
        own = 4.0 * dot3(split(z_half), split(y_half), 0)
        t_column, t_row = diagonals(own)
        it_row = lax.rsqrt(t_row)
        t_rows.append(t_row)
        z_unit = z_half * it_row
        zs.append(z_unit)
        its.append(own * lax.rsqrt(t_column) * it_row)
        ul.append(split(z_unit * roots_columns[n]))
    diag2 = jnp.concatenate([half_of(diag_rows[n], second[n], 1) * t_rows[n] for n in range(2)], axis=1)
    ends = math.sqrt(0.5) * jnp.sqrt(0.5 * diag2)
    root_row = lax.rsqrt(diag_rows[1])

    gc.wait_send()
    cc.wait_send()
    wait_for(cross_parts, cz_send)
    wait_for(cross_parts, ca_send)

    def own_sent(gz_rows, ga_rows):
        wait_for(grams.at[0, pl.ds(0, gz_rows)], gz_send)
        wait_for(grams.at[0, pl.ds(0, ga_rows)], ga_send)

    others = z_devices - 1
    either(
        z == 0,
        lambda: own_sent(others * g_part, others * (g_part + 8)),
        lambda: own_sent(others * g_part + 8, others * g_part),
    )
    wait_for(grams.at[0], across_send)
    for n, (edge, copy) in enumerate(((is_last, x_up), (is_first, x_down))):

        @pl.when(jnp.logical_not(edge))
        def _(n=n, copy=copy):
            copy.wait_send()
            wait_for(gram_full, straight_send.at[n])

    z_rows = split(half_of(zs[0], core == 1, 0))
    z_other = split(zs[1])
    roots_half = half_of(roots_columns[0], core == 1, 0)
    wait_for(cross, ca_recv)
    turned = dot3(split(cross[...] * roots_half * root_row), z_other)
    mixed_local[...] = dot3(z_rows, split(turned), 0)
    cf = remote(mixed_local, mixed_core, cf_send, cf_recv, sibling)
    cf.start()
    cf.wait_recv()
    off = mixed_local[...] + mixed_core[...]
    scaled2 = jnp.concatenate(
        [jnp.concatenate([its[0], off], axis=1), jnp.concatenate([off.T, its[1]], axis=1)], axis=0
    )
    last = Solve([scaled2])
    last.step()
    ul = [split(dot3(moved_split[n], ul[n])) for n in range(2)]
    ul = [jnp.concatenate([ul[0][p], ul[1][p]], axis=1) for p in range(2)]
    for _ in range(NSTEPS - 3):
        last.step()
    last.factors()
    almost = dot3(ul, last.z_split[0])
    out_ref[...] = dot3(split(almost), last.f[0]) * ends
    cf.wait_send()


def shards(blk_devices, z_devices, x):
    rows, width = x.shape
    half = width // 2
    dma = pltpu.SemaphoreType.DMA
    g_half, c_half = half + 8, width // 2
    g_part = half // z_devices + 8
    others = z_devices - 1
    vmem = lambda *shape: pltpu.VMEM(shape, jnp.float32)
    return pl.pallas_call(
        functools.partial(kernel, blk_devices, z_devices),
        out_shape=jax.ShapeDtypeStruct(x.shape, jnp.float32),
        in_specs=[pl.BlockSpec(memory_space=pltpu.MemorySpace.HBM)],
        out_specs=pl.BlockSpec(memory_space=pltpu.VMEM),
        scratch_shapes=[
            vmem(rows, width), vmem(2, rows, width),
            vmem(2 * g_half, half), vmem(g_half, half), vmem(g_half, half),
            vmem(others, g_part, half), vmem(g_part, half), vmem(g_half, half), vmem(2, 2 * g_half, half),
            vmem(c_half, width), vmem(c_half, width), vmem(c_half, width),
            vmem(others, c_half // z_devices, width), vmem(c_half // z_devices, width), vmem(c_half, width),
            vmem(half, half), vmem(half, half),
            pltpu.SemaphoreType.REGULAR((others,)), dma, dma((2,)), dma((2,)), dma, dma, dma, dma, dma, dma((2,)),
            dma((2,)), dma, dma((2,)), dma, dma, dma, dma, dma, dma, dma, dma,
        ],
        compiler_params=pltpu.CompilerParams(
            collective_id=0, has_side_effects=True, vmem_limit_bytes=32 * 1024 * 1024
        ),
        cost_estimate=pl.CostEstimate(
            flops=40 * 3 * 2 * width**3, bytes_accessed=8 * rows * width, transcendentals=4096
        ),
        name="rotate_pairs",
    )(pltpu.with_memory_space_constraint(x, pltpu.MemorySpace.HBM))


def solution(mesh):
    run = functools.partial(shards, mesh.shape["blk"], mesh.shape["row"] // 2)
    return jax.shard_map(
        run, mesh=mesh, in_specs=(P("row", "blk"),), out_specs=P("row", "blk"), check_vma=False
    )
```

```python
import functools
import math

import jax
import jax.numpy as jnp
from jax import lax
from jax.experimental import pallas as pl
from jax.experimental.pallas import tpu as pltpu
from jax.sharding import PartitionSpec as P

NSTEPS = 5
MESH = pl.DeviceIdType.MESH


def product(a, b, lhs_dim=1):
    return lax.dot_general(
        a, b, (((lhs_dim,), (0,)), ((), ())), preferred_element_type=jnp.float32
    )


def split(a):
    high = a.astype(jnp.bfloat16)
    return high, (a - high.astype(jnp.float32)).astype(jnp.bfloat16)


def dot3(a, b, lhs_dim=1):
    high, low = a
    if lhs_dim == 0:
        return product(high, b[0], 0) + (product(high, b[1], 0) + product(low, b[0], 0))
    half = high.shape[0] // 2
    blocks = []
    for rows in (slice(0, half), slice(half, 2 * half)):
        small = product(high[rows], b[1]) + product(low[rows], b[0])
        blocks.append(product(high[rows], b[0]) + small)
    return jnp.concatenate(blocks, axis=0)


def eye(n):
    rows = lax.broadcasted_iota(jnp.int32, (n, n), 0)
    columns = lax.broadcasted_iota(jnp.int32, (n, n), 1)
    return rows == columns


def diagonals(a):
    kept = jnp.where(eye(a.shape[0]), a, 0.0)
    return jnp.sum(kept, axis=1, keepdims=True), jnp.sum(kept, axis=0, keepdims=True)


class Solve:
    def __init__(self, starts):
        self.eye = jnp.where(eye(starts[0].shape[0]), 1.5, 0.0)
        y = [0.25 * m for m in starts]
        self.z = [self.eye - m for m in y]
        self.f = self.z_split = [split(z) for z in self.z]
        self.y = [dot3(f, split(m)) for f, m in zip(self.f, y)]
        self.y_split = [split(m) for m in self.y]

    def factors(self):
        self.f = [split(self.eye - dot3(y, z)) for y, z in zip(self.y_split, self.z_split)]

    def step(self):
        self.factors()
        self.z = [dot3(f, z) for f, z in zip(self.f, self.z_split)]
        self.z_split = [split(z) for z in self.z]
        self.y = [dot3(f, y) for f, y in zip(self.f, self.y_split)]
        self.y_split = [split(y) for y in self.y]


def half_of(a, second, axis):
    n = a.shape[axis] // 2
    first = lax.slice_in_dim(a, 0, n, axis=axis)
    return jnp.where(second, lax.slice_in_dim(a, n, 2 * n, axis=axis), first)


def kernel(
    blk_devices, z_devices,
    x_hbm, out_ref,
    x_ref, moved, gram_local, gram_core, gram_sum, gram_parts, gram_shard, gram_full, grams,
    cross_local, cross_core, cross_sum, cross_parts, cross_shard, cross, mixed_local, mixed_core,
    here_sem, load_sem, x_send, x_recv, gc_send, gc_recv, gz_send, gz_recv, ga_send, ga_recv,
    straight_send, across_send, gx_recv, cc_send, cc_recv, cz_send, cz_recv, ca_send, ca_recv, cf_send, cf_recv,
):
    k = lax.axis_index("blk")
    row = lax.axis_index("row")
    z = row // 2
    core = row % 2
    is_first = k == 0
    is_last = k == blk_devices - 1
    up = jnp.minimum(k + 1, blk_devices - 1)
    down = jnp.maximum(k - 1, 0)
    up_slot = jnp.where(is_last, 1, 0)
    down_slot = jnp.where(is_first, 0, 1)
    second = (k == 1, jnp.logical_not(is_last))
    half_width = x_ref.shape[1] // 2
    g_half = gram_local.shape[0] // 2
    g_part = half_width // z_devices
    g_parts = [(0, g_part + 8)] + [(8 + n * g_part, g_part) for n in range(1, z_devices)]
    c_half = cross_local.shape[0]
    c_part = c_half // z_devices
    middle = z_devices // 2
    lower_side = z < middle
    far_first = sorted(range(1, z_devices), key=lambda t: -min(t, z_devices - t))

    def peer(blk, t, other=False):
        return {"blk": blk, "row": lax.rem(z + t, z_devices) * 2 + (1 - core if other else core)}

    sibling = peer(k, 0, True)

    def remote(src, dst, send, recv, device):
        return pltpu.make_async_remote_copy(
            src_ref=src, dst_ref=dst, send_sem=send, recv_sem=recv,
            device_id=device, device_id_type=MESH,
        )

    def wait_for(ref, sem):
        pltpu.make_async_copy(ref, ref, sem).wait()

    def rows_at(start, size):
        return pl.ds(pl.multiple_of(start, 8), size)

    def either(condition, yes, no):
        pl.when(condition)(lambda: yes() and None)
        pl.when(jnp.logical_not(condition))(lambda: no() and None)

    def signal(sem, device):
        pl.semaphore_signal(sem, inc=1, device_id=device, device_id_type=MESH)

    load = pltpu.make_async_copy(x_hbm, x_ref, load_sem)
    load.start()

    barrier = pltpu.get_barrier_semaphore()
    for edge, blk in ((is_last, up), (is_first, down)):
        for other in (False, True):
            pl.when(jnp.logical_not(edge))(functools.partial(signal, barrier, peer(blk, 0, other)))
    signal(barrier, sibling)
    for t in range(z_devices - 1, 0, -1):
        pl.when(z + t < z_devices)(functools.partial(signal, barrier, peer(k, t)))
    neighbours = 2 - is_first.astype(jnp.int32) - is_last.astype(jnp.int32)

    load.wait()
    x_split = split(x_ref[...])
    g = dot3(x_split, x_split, 0)
    block_rows = lax.broadcasted_iota(jnp.int32, (half_width, half_width), 0)
    block_columns = lax.broadcasted_iota(jnp.int32, (half_width, half_width), 1)
    gram_local[:half_width] = g[:half_width, half_width:]
    gram_local[half_width:g_half] = jnp.zeros((8, half_width), jnp.float32)
    gram_local[g_half : g_half + half_width] = jnp.where(
        block_rows >= block_columns, g[:half_width, :half_width], g[half_width:, half_width:]
    )
    gram_local[g_half + half_width :] = jnp.broadcast_to(diagonals(g[half_width:, half_width:])[1], (8, half_width))

    pl.semaphore_wait(barrier, z + 1 + 2 * neighbours)

    for t in range(z_devices - 1, 0, -1):
        pl.when(z - t >= 0)(functools.partial(signal, here_sem.at[t - 1], peer(k, z_devices - t)))

    gc = remote(gram_local.at[rows_at((1 - core) * g_half, g_half)], gram_core, gc_send, gc_recv, sibling)
    gc.start()

    x_up = remote(x_ref, moved.at[up_slot], x_send.at[0], x_recv.at[up_slot], peer(up, 0))
    x_down = remote(x_ref, moved.at[down_slot], x_send.at[1], x_recv.at[down_slot], peer(down, 0))
    either(is_last, pltpu.make_async_copy(x_ref, moved.at[1], x_recv.at[1]).start, x_up.start)
    either(is_first, pltpu.make_async_copy(x_ref, moved.at[0], x_recv.at[0]).start, x_down.start)


    def to_others(src, dst, send, recv):
        for there in range(z_devices):
            copy = remote(src, dst, send, recv, {"blk": k, "row": there * 2 + core})
            pl.when(z != there)(copy.start)

    def tree(terms):
        while len(terms) > 1:
            terms = [a + b for a, b in zip(terms[::2], terms[1::2])]
        return terms[0]

    gc.wait_recv()
    gram_sum[...] = gram_local[rows_at(core * g_half, g_half)] + gram_core[...]
    for owner in sorted(range(z_devices), key=lambda n: -min(n, z_devices - n)):

        @pl.when(z < owner)
        def _(owner=owner):
            pl.semaphore_wait(here_sem.at[owner - z - 1], 1)

        t = lax.rem(owner - z + z_devices, z_devices)
        start, size = g_parts[owner]
        copy = remote(
            gram_sum.at[pl.ds(start, size)], gram_parts.at[jnp.maximum(t - 1, 0), pl.ds(0, size)], gz_send, gz_recv,
            {"blk": k, "row": owner * 2 + core},
        )
        pl.when(z != owner)(copy.start)

    def own_part(start, size):
        wait_for(grams.at[0, pl.ds(0, (z_devices - 1) * size)], gz_recv)
        gram_shard[:size] = tree(
            [gram_sum[pl.ds(start, size)]] + [gram_parts[n, :size] for n in range(z_devices - 1)]
        )
        src, dst = gram_shard.at[pl.ds(0, size)], gram_full.at[pl.ds(start, size)]
        sem = ga_recv.at[jnp.where(lower_side, 0, 1)]
        pltpu.make_async_copy(src, dst, sem).start()
        to_others(src, dst, ga_send, sem)

    cc = remote(cross_local, cross_core, cc_send, cc_recv, sibling)

    def gram_sum_part():
        either(
            z == 0,
            functools.partial(own_part, *g_parts[0]),
            lambda: own_part(pl.multiple_of(8 + z * g_part, 8), g_part),
        )

    def cross_part():
        for slot in range(2):
            wait_for(moved.at[slot], x_recv.at[slot])
        b_split = split(moved[1])
        a_half = [half_of(moved[0], core == which, 1) for which in (0, 1)]
        cross_local[...] = dot3(split(a_half[0]), b_split, 0)
        cc.start()
        cross_sum[...] = dot3(split(a_half[1]), b_split, 0)
    either(
        lower_side,
        lambda: (cross_part(), gram_sum_part()),
        lambda: (gram_sum_part(), cross_part()),
    )

    cc.wait_recv()
    cross_sum[...] += cross_core[...]
    for owner in sorted(range(z_devices), key=lambda n: -min(n, z_devices - n)):
        t = lax.rem(owner - z + z_devices, z_devices)
        copy = remote(
            cross_sum.at[pl.ds(owner * c_part, c_part)], cross_parts.at[jnp.maximum(t - 1, 0)], cz_send, cz_recv,
            {"blk": k, "row": owner * 2 + core},
        )
        pl.when(z != owner)(copy.start)

    def forward(side):
        start = g_parts[side * middle][0]
        size = (g_parts[middle][0], g_half - g_parts[middle][0])[side]
        src = gram_full.at[pl.ds(start, size)]
        there = rows_at(core * g_half + start, size)
        wait_for(src, ga_recv.at[side])
        for n, (edge, blk, slot, own_slot) in enumerate(((is_last, up, up_slot, 1), (is_first, down, down_slot, 0))):
            dst = grams.at[slot, there]
            straight = remote(src, dst, straight_send.at[n], gx_recv.at[slot], peer(blk, 0))
            stays = pltpu.make_async_copy(src, grams.at[own_slot, there], gx_recv.at[own_slot])
            either(edge, stays.start, straight.start)
            remote(src, dst, across_send, gx_recv.at[slot], peer(blk, 0, True)).start()

    either(lower_side, lambda: (forward(0), forward(1)), lambda: (forward(1), forward(0)))

    wait_for(cross_parts, cz_recv)
    cross_shard[...] = tree([cross_sum[rows_at(z * c_part, c_part)]] + [cross_parts[n] for n in range(z_devices - 1)])
    c_mine = rows_at(z * c_part, c_part)
    to_others(cross_shard, cross.at[c_mine], ca_send, ca_recv)
    pltpu.make_async_copy(cross_shard, cross.at[c_mine], ca_recv).start()

    for slot in range(2):
        wait_for(grams.at[slot], gx_recv.at[slot])
    diag_rows, roots_columns, scaled = [], [], []
    for slot in range(2):
        upper = grams[slot, pl.ds(0, half_width)]
        packed = grams[slot, pl.ds(g_half, half_width)]
        corner = jnp.where(block_rows < block_columns, packed, packed.T)
        corner = jnp.where(block_rows == block_columns, grams[slot, pl.ds(g_half + half_width, 1)], corner)
        full = jnp.concatenate(
            [
                jnp.concatenate([jnp.where(block_rows >= block_columns, packed, packed.T), upper], axis=1),
                jnp.concatenate([upper.T, corner], axis=1),
            ],
            axis=0,
        )
        column, line = diagonals(full)
        diag_rows.append(line)
        roots_columns.append(lax.rsqrt(column))
        scaled.append(full * roots_columns[slot] * lax.rsqrt(line))
    first = Solve(scaled)
    for _ in range(NSTEPS - 2):
        first.step()
    first.factors()
    zs, t_rows, its, ul = [], [], [], []
    moved_split = [split(moved[slot]) for slot in range(2)]
    for n in range(2):
        z_half = dot3(first.f[n], split(half_of(first.z[n], second[n], 1)))
        y_half = dot3(first.f[n], split(half_of(first.y[n], second[n], 1)))
        own = 4.0 * dot3(split(z_half), split(y_half), 0)
        t_column, t_row = diagonals(own)
        it_row = lax.rsqrt(t_row)
        t_rows.append(t_row)
        z_unit = z_half * it_row
        zs.append(z_unit)
        its.append(own * lax.rsqrt(t_column) * it_row)
        ul.append(split(z_unit * roots_columns[n]))
    diag2 = jnp.concatenate([half_of(diag_rows[n], second[n], 1) * t_rows[n] for n in range(2)], axis=1)
    ends = math.sqrt(0.5) * jnp.sqrt(0.5 * diag2)
    root_row = lax.rsqrt(diag_rows[1])

    gc.wait_send()
    cc.wait_send()
    wait_for(cross_parts, cz_send)
    wait_for(cross_parts, ca_send)

    def own_sent(gz_rows, ga_rows):
        wait_for(grams.at[0, pl.ds(0, gz_rows)], gz_send)
        wait_for(grams.at[0, pl.ds(0, ga_rows)], ga_send)

    others = z_devices - 1
    either(
        z == 0,
        lambda: own_sent(others * g_part, others * (g_part + 8)),
        lambda: own_sent(others * g_part + 8, others * g_part),
    )
    wait_for(grams.at[0], across_send)
    for n, (edge, copy) in enumerate(((is_last, x_up), (is_first, x_down))):

        @pl.when(jnp.logical_not(edge))
        def _(n=n, copy=copy):
            copy.wait_send()
            wait_for(gram_full, straight_send.at[n])

    z_rows = split(half_of(zs[0], core == 1, 0))
    z_other = split(zs[1])
    roots_half = half_of(roots_columns[0], core == 1, 0)
    wait_for(cross, ca_recv)
    turned = dot3(split(cross[...] * roots_half * root_row), z_other)
    mixed_local[...] = dot3(z_rows, split(turned), 0)
    cf = remote(mixed_local, mixed_core, cf_send, cf_recv, sibling)
    cf.start()
    cf.wait_recv()
    off = mixed_local[...] + mixed_core[...]
    scaled2 = jnp.concatenate(
        [jnp.concatenate([its[0], off], axis=1), jnp.concatenate([off.T, its[1]], axis=1)], axis=0
    )
    last = Solve([scaled2])
    last.step()
    ul = [split(dot3(moved_split[n], ul[n])) for n in range(2)]
    ul = [jnp.concatenate([ul[0][p], ul[1][p]], axis=1) for p in range(2)]
    for _ in range(NSTEPS - 3):
        last.step()
    last.factors()
    almost = dot3(ul, last.z_split[0])
    out_ref[...] = dot3(split(almost), last.f[0]) * ends
    cf.wait_send()


def shards(blk_devices, z_devices, x):
    rows, width = x.shape
    half = width // 2
    dma = pltpu.SemaphoreType.DMA
    g_half, c_half = half + 8, width // 2
    g_part = half // z_devices + 8
    others = z_devices - 1
    vmem = lambda *shape: pltpu.VMEM(shape, jnp.float32)
    return pl.pallas_call(
        functools.partial(kernel, blk_devices, z_devices),
        out_shape=jax.ShapeDtypeStruct(x.shape, jnp.float32),
        in_specs=[pl.BlockSpec(memory_space=pltpu.MemorySpace.HBM)],
        out_specs=pl.BlockSpec(memory_space=pltpu.VMEM),
        scratch_shapes=[
            vmem(rows, width), vmem(2, rows, width),
            vmem(2 * g_half, half), vmem(g_half, half), vmem(g_half, half),
            vmem(others, g_part, half), vmem(g_part, half), vmem(g_half, half), vmem(2, 2 * g_half, half),
            vmem(c_half, width), vmem(c_half, width), vmem(c_half, width),
            vmem(others, c_half // z_devices, width), vmem(c_half // z_devices, width), vmem(c_half, width),
            vmem(half, half), vmem(half, half),
            pltpu.SemaphoreType.REGULAR((others,)), dma, dma((2,)), dma((2,)), dma, dma, dma, dma, dma, dma((2,)),
            dma((2,)), dma, dma((2,)), dma, dma, dma, dma, dma, dma, dma, dma,
        ],
        compiler_params=pltpu.CompilerParams(
            collective_id=0, has_side_effects=True, vmem_limit_bytes=32 * 1024 * 1024
        ),
        cost_estimate=pl.CostEstimate(
            flops=40 * 3 * 2 * width**3, bytes_accessed=8 * rows * width, transcendentals=4096
        ),
        name="rotate_pairs",
    )(pltpu.with_memory_space_constraint(x, pltpu.MemorySpace.HBM))


def solution(mesh):
    run = functools.partial(shards, mesh.shape["blk"], mesh.shape["row"] // 2)
    return jax.shard_map(
        run, mesh=mesh, in_specs=(P("row", "blk"),), out_specs=P("row", "blk"), check_vma=False
    )
```

```python
import functools
import math

import jax
import jax.numpy as jnp
from jax import lax
from jax.experimental import pallas as pl
from jax.experimental.pallas import tpu as pltpu
from jax.sharding import PartitionSpec as P

NSTEPS = 5
MESH = pl.DeviceIdType.MESH


def product(a, b, lhs_dim=1):
    return lax.dot_general(
        a, b, (((lhs_dim,), (0,)), ((), ())), preferred_element_type=jnp.float32
    )


def split(a):
    high = a.astype(jnp.bfloat16)
    return high, (a - high.astype(jnp.float32)).astype(jnp.bfloat16)


def dot3(a, b, lhs_dim=1):
    high, low = a
    if lhs_dim == 0:
        return product(high, b[0], 0) + (product(high, b[1], 0) + product(low, b[0], 0))
    half = high.shape[0] // 2
    blocks = []
    for rows in (slice(0, half), slice(half, 2 * half)):
        both = product(jnp.concatenate([high[rows], low[rows]], axis=0), b[0])
        blocks.append(both[:half] + (both[half:] + product(high[rows], b[1])))
    return jnp.concatenate(blocks, axis=0)


def eye(n):
    rows = lax.broadcasted_iota(jnp.int32, (n, n), 0)
    columns = lax.broadcasted_iota(jnp.int32, (n, n), 1)
    return rows == columns


def diagonals(a):
    kept = jnp.where(eye(a.shape[0]), a, 0.0)
    return jnp.sum(kept, axis=1, keepdims=True), jnp.sum(kept, axis=0, keepdims=True)


class Solve:
    def __init__(self, starts):
        self.eye = jnp.where(eye(starts[0].shape[0]), 1.5, 0.0)
        y = [0.25 * m for m in starts]
        self.z = [self.eye - m for m in y]
        self.f = self.z_split = [split(z) for z in self.z]
        self.y = [dot3(f, split(m)) for f, m in zip(self.f, y)]
        self.y_split = [split(m) for m in self.y]

    def factors(self):
        self.f = [split(self.eye - dot3(y, z)) for y, z in zip(self.y_split, self.z_split)]

    def step(self):
        self.factors()
        self.z = [dot3(f, z) for f, z in zip(self.f, self.z_split)]
        self.z_split = [split(z) for z in self.z]
        self.y = [dot3(f, y) for f, y in zip(self.f, self.y_split)]
        self.y_split = [split(y) for y in self.y]


def half_of(a, second, axis):
    n = a.shape[axis] // 2
    first = lax.slice_in_dim(a, 0, n, axis=axis)
    return jnp.where(second, lax.slice_in_dim(a, n, 2 * n, axis=axis), first)


def kernel(
    blk_devices, z_devices,
    x_hbm, out_ref,
    x_ref, moved, gram_local, gram_core, gram_sum, gram_parts, gram_shard, gram_full, grams,
    cross_local, cross_core, cross_sum, cross_parts, cross_shard, cross, mixed_local, mixed_core,
    here_sem, load_sem, x_send, x_recv, gc_send, gc_recv, gz_send, gz_recv, ga_send, ga_recv,
    straight_send, across_send, gx_recv, cc_send, cc_recv, cz_send, cz_recv, ca_send, ca_recv, cf_send, cf_recv,
):
    k = lax.axis_index("blk")
    row = lax.axis_index("row")
    z = row // 2
    core = row % 2
    is_first = k == 0
    is_last = k == blk_devices - 1
    up = jnp.minimum(k + 1, blk_devices - 1)
    down = jnp.maximum(k - 1, 0)
    up_slot = jnp.where(is_last, 1, 0)
    down_slot = jnp.where(is_first, 0, 1)
    second = (k == 1, jnp.logical_not(is_last))
    half_width = x_ref.shape[1] // 2
    g_half = gram_local.shape[0] // 2
    g_part = half_width // z_devices
    g_parts = [(0, g_part + 8)] + [(8 + n * g_part, g_part) for n in range(1, z_devices)]
    c_half = cross_local.shape[0]
    c_part = c_half // z_devices
    middle = z_devices // 2
    lower_side = z < middle
    far_first = sorted(range(1, z_devices), key=lambda t: -min(t, z_devices - t))

    def peer(blk, t, other=False):
        return {"blk": blk, "row": lax.rem(z + t, z_devices) * 2 + (1 - core if other else core)}

    sibling = peer(k, 0, True)

    def remote(src, dst, send, recv, device):
        return pltpu.make_async_remote_copy(
            src_ref=src, dst_ref=dst, send_sem=send, recv_sem=recv,
            device_id=device, device_id_type=MESH,
        )

    def wait_for(ref, sem):
        pltpu.make_async_copy(ref, ref, sem).wait()

    def rows_at(start, size):
        return pl.ds(pl.multiple_of(start, 8), size)

    def either(condition, yes, no):
        pl.when(condition)(lambda: yes() and None)
        pl.when(jnp.logical_not(condition))(lambda: no() and None)

    def signal(sem, device):
        pl.semaphore_signal(sem, inc=1, device_id=device, device_id_type=MESH)

    load = pltpu.make_async_copy(x_hbm, x_ref, load_sem)
    load.start()

    barrier = pltpu.get_barrier_semaphore()
    for edge, blk in ((is_last, up), (is_first, down)):
        for other in (False, True):
            pl.when(jnp.logical_not(edge))(functools.partial(signal, barrier, peer(blk, 0, other)))
    signal(barrier, sibling)
    for t in range(z_devices - 1, 0, -1):
        pl.when(z + t < z_devices)(functools.partial(signal, barrier, peer(k, t)))
    neighbours = 2 - is_first.astype(jnp.int32) - is_last.astype(jnp.int32)

    load.wait()
    x_split = split(x_ref[...])
    g = dot3(x_split, x_split, 0)
    block_rows = lax.broadcasted_iota(jnp.int32, (half_width, half_width), 0)
    block_columns = lax.broadcasted_iota(jnp.int32, (half_width, half_width), 1)
    gram_local[:half_width] = g[:half_width, half_width:]
    gram_local[half_width:g_half] = jnp.zeros((8, half_width), jnp.float32)
    gram_local[g_half : g_half + half_width] = jnp.where(
        block_rows >= block_columns, g[:half_width, :half_width], g[half_width:, half_width:]
    )
    gram_local[g_half + half_width :] = jnp.broadcast_to(diagonals(g[half_width:, half_width:])[1], (8, half_width))

    pl.semaphore_wait(barrier, z + 1 + 2 * neighbours)

    for t in range(z_devices - 1, 0, -1):
        pl.when(z - t >= 0)(functools.partial(signal, here_sem.at[t - 1], peer(k, z_devices - t)))

    gc = remote(gram_local.at[rows_at((1 - core) * g_half, g_half)], gram_core, gc_send, gc_recv, sibling)
    gc.start()

    x_up = remote(x_ref, moved.at[up_slot], x_send.at[0], x_recv.at[up_slot], peer(up, 0))
    x_down = remote(x_ref, moved.at[down_slot], x_send.at[1], x_recv.at[down_slot], peer(down, 0))
    either(is_last, pltpu.make_async_copy(x_ref, moved.at[1], x_recv.at[1]).start, x_up.start)
    either(is_first, pltpu.make_async_copy(x_ref, moved.at[0], x_recv.at[0]).start, x_down.start)


    def to_others(src, dst, send, recv):
        for there in range(z_devices):
            copy = remote(src, dst, send, recv, {"blk": k, "row": there * 2 + core})
            pl.when(z != there)(copy.start)

    def tree(terms):
        while len(terms) > 1:
            terms = [a + b for a, b in zip(terms[::2], terms[1::2])]
        return terms[0]

    gc.wait_recv()
    gram_sum[...] = gram_local[rows_at(core * g_half, g_half)] + gram_core[...]
    for owner in sorted(range(z_devices), key=lambda n: -min(n, z_devices - n)):

        @pl.when(z < owner)
        def _(owner=owner):
            pl.semaphore_wait(here_sem.at[owner - z - 1], 1)

        t = lax.rem(owner - z + z_devices, z_devices)
        start, size = g_parts[owner]
        copy = remote(
            gram_sum.at[pl.ds(start, size)], gram_parts.at[jnp.maximum(t - 1, 0), pl.ds(0, size)], gz_send, gz_recv,
            {"blk": k, "row": owner * 2 + core},
        )
        pl.when(z != owner)(copy.start)

    def own_part(start, size):
        wait_for(grams.at[0, pl.ds(0, (z_devices - 1) * size)], gz_recv)
        gram_shard[:size] = tree(
            [gram_sum[pl.ds(start, size)]] + [gram_parts[n, :size] for n in range(z_devices - 1)]
        )
        src, dst = gram_shard.at[pl.ds(0, size)], gram_full.at[pl.ds(start, size)]
        sem = ga_recv.at[jnp.where(lower_side, 0, 1)]
        pltpu.make_async_copy(src, dst, sem).start()
        to_others(src, dst, ga_send, sem)

    cc = remote(cross_local, cross_core, cc_send, cc_recv, sibling)

    def gram_sum_part():
        either(
            z == 0,
            functools.partial(own_part, *g_parts[0]),
            lambda: own_part(pl.multiple_of(8 + z * g_part, 8), g_part),
        )

    def cross_part():
        for slot in range(2):
            wait_for(moved.at[slot], x_recv.at[slot])
        b_split = split(moved[1])
        a_half = [half_of(moved[0], core == which, 1) for which in (0, 1)]
        cross_local[...] = dot3(split(a_half[0]), b_split, 0)
        cc.start()
        cross_sum[...] = dot3(split(a_half[1]), b_split, 0)
    either(
        lower_side,
        lambda: (cross_part(), gram_sum_part()),
        lambda: (gram_sum_part(), cross_part()),
    )

    cc.wait_recv()
    cross_sum[...] += cross_core[...]
    for owner in sorted(range(z_devices), key=lambda n: -min(n, z_devices - n)):
        t = lax.rem(owner - z + z_devices, z_devices)
        copy = remote(
            cross_sum.at[pl.ds(owner * c_part, c_part)], cross_parts.at[jnp.maximum(t - 1, 0)], cz_send, cz_recv,
            {"blk": k, "row": owner * 2 + core},
        )
        pl.when(z != owner)(copy.start)

    def forward(side):
        start = g_parts[side * middle][0]
        size = (g_parts[middle][0], g_half - g_parts[middle][0])[side]
        src = gram_full.at[pl.ds(start, size)]
        there = rows_at(core * g_half + start, size)
        wait_for(src, ga_recv.at[side])
        for n, (edge, blk, slot, own_slot) in enumerate(((is_last, up, up_slot, 1), (is_first, down, down_slot, 0))):
            dst = grams.at[slot, there]
            straight = remote(src, dst, straight_send.at[n], gx_recv.at[slot], peer(blk, 0))
            stays = pltpu.make_async_copy(src, grams.at[own_slot, there], gx_recv.at[own_slot])
            either(edge, stays.start, straight.start)
            remote(src, dst, across_send, gx_recv.at[slot], peer(blk, 0, True)).start()

    either(lower_side, lambda: (forward(0), forward(1)), lambda: (forward(1), forward(0)))

    wait_for(cross_parts, cz_recv)
    cross_shard[...] = tree([cross_sum[rows_at(z * c_part, c_part)]] + [cross_parts[n] for n in range(z_devices - 1)])
    c_mine = rows_at(z * c_part, c_part)
    to_others(cross_shard, cross.at[c_mine], ca_send, ca_recv)
    pltpu.make_async_copy(cross_shard, cross.at[c_mine], ca_recv).start()

    for slot in range(2):
        wait_for(grams.at[slot], gx_recv.at[slot])
    diag_rows, roots_columns, scaled = [], [], []
    for slot in range(2):
        upper = grams[slot, pl.ds(0, half_width)]
        packed = grams[slot, pl.ds(g_half, half_width)]
        corner = jnp.where(block_rows < block_columns, packed, packed.T)
        corner = jnp.where(block_rows == block_columns, grams[slot, pl.ds(g_half + half_width, 1)], corner)
        full = jnp.concatenate(
            [
                jnp.concatenate([jnp.where(block_rows >= block_columns, packed, packed.T), upper], axis=1),
                jnp.concatenate([upper.T, corner], axis=1),
            ],
            axis=0,
        )
        column, line = diagonals(full)
        diag_rows.append(line)
        roots_columns.append(lax.rsqrt(column))
        scaled.append(full * roots_columns[slot] * lax.rsqrt(line))
    first = Solve(scaled)
    for _ in range(NSTEPS - 2):
        first.step()
    first.factors()
    zs, t_rows, its, ul = [], [], [], []
    moved_split = [split(moved[slot]) for slot in range(2)]
    for n in range(2):
        z_half = dot3(first.f[n], split(half_of(first.z[n], second[n], 1)))
        y_half = dot3(first.f[n], split(half_of(first.y[n], second[n], 1)))
        own = 4.0 * dot3(split(z_half), split(y_half), 0)
        t_column, t_row = diagonals(own)
        it_row = lax.rsqrt(t_row)
        t_rows.append(t_row)
        z_unit = z_half * it_row
        zs.append(z_unit)
        its.append(own * lax.rsqrt(t_column) * it_row)
        ul.append(split(z_unit * roots_columns[n]))
    diag2 = jnp.concatenate([half_of(diag_rows[n], second[n], 1) * t_rows[n] for n in range(2)], axis=1)
    ends = math.sqrt(0.5) * jnp.sqrt(0.5 * diag2)
    root_row = lax.rsqrt(diag_rows[1])

    gc.wait_send()
    cc.wait_send()
    wait_for(cross_parts, cz_send)
    wait_for(cross_parts, ca_send)

    def own_sent(gz_rows, ga_rows):
        wait_for(grams.at[0, pl.ds(0, gz_rows)], gz_send)
        wait_for(grams.at[0, pl.ds(0, ga_rows)], ga_send)

    others = z_devices - 1
    either(
        z == 0,
        lambda: own_sent(others * g_part, others * (g_part + 8)),
        lambda: own_sent(others * g_part + 8, others * g_part),
    )
    wait_for(grams.at[0], across_send)
    for n, (edge, copy) in enumerate(((is_last, x_up), (is_first, x_down))):

        @pl.when(jnp.logical_not(edge))
        def _(n=n, copy=copy):
            copy.wait_send()
            wait_for(gram_full, straight_send.at[n])

    z_rows = split(half_of(zs[0], core == 1, 0))
    z_other = split(zs[1])
    roots_half = half_of(roots_columns[0], core == 1, 0)
    wait_for(cross, ca_recv)
    turned = dot3(split(cross[...] * roots_half * root_row), z_other)
    mixed_local[...] = dot3(z_rows, split(turned), 0)
    cf = remote(mixed_local, mixed_core, cf_send, cf_recv, sibling)
    cf.start()
    cf.wait_recv()
    off = mixed_local[...] + mixed_core[...]
    scaled2 = jnp.concatenate(
        [jnp.concatenate([its[0], off], axis=1), jnp.concatenate([off.T, its[1]], axis=1)], axis=0
    )
    last = Solve([scaled2])
    last.step()
    ul = [split(dot3(moved_split[n], ul[n])) for n in range(2)]
    ul = [jnp.concatenate([ul[0][p], ul[1][p]], axis=1) for p in range(2)]
    for _ in range(NSTEPS - 3):
        last.step()
    last.factors()
    almost = dot3(ul, last.z_split[0])
    out_ref[...] = dot3(split(almost), last.f[0]) * ends
    cf.wait_send()


def shards(blk_devices, z_devices, x):
    rows, width = x.shape
    half = width // 2
    dma = pltpu.SemaphoreType.DMA
    g_half, c_half = half + 8, width // 2
    g_part = half // z_devices + 8
    others = z_devices - 1
    vmem = lambda *shape: pltpu.VMEM(shape, jnp.float32)
    return pl.pallas_call(
        functools.partial(kernel, blk_devices, z_devices),
        out_shape=jax.ShapeDtypeStruct(x.shape, jnp.float32),
        in_specs=[pl.BlockSpec(memory_space=pltpu.MemorySpace.HBM)],
        out_specs=pl.BlockSpec(memory_space=pltpu.VMEM),
        scratch_shapes=[
            vmem(rows, width), vmem(2, rows, width),
            vmem(2 * g_half, half), vmem(g_half, half), vmem(g_half, half),
            vmem(others, g_part, half), vmem(g_part, half), vmem(g_half, half), vmem(2, 2 * g_half, half),
            vmem(c_half, width), vmem(c_half, width), vmem(c_half, width),
            vmem(others, c_half // z_devices, width), vmem(c_half // z_devices, width), vmem(c_half, width),
            vmem(half, half), vmem(half, half),
            pltpu.SemaphoreType.REGULAR((others,)), dma, dma((2,)), dma((2,)), dma, dma, dma, dma, dma, dma((2,)),
            dma((2,)), dma, dma((2,)), dma, dma, dma, dma, dma, dma, dma, dma,
        ],
        compiler_params=pltpu.CompilerParams(
            collective_id=0, has_side_effects=True, vmem_limit_bytes=32 * 1024 * 1024
        ),
        cost_estimate=pl.CostEstimate(
            flops=40 * 3 * 2 * width**3, bytes_accessed=8 * rows * width, transcendentals=4096
        ),
        name="rotate_pairs",
    )(pltpu.with_memory_space_constraint(x, pltpu.MemorySpace.HBM))


def solution(mesh):
    run = functools.partial(shards, mesh.shape["blk"], mesh.shape["row"] // 2)
    return jax.shard_map(
        run, mesh=mesh, in_specs=(P("row", "blk"),), out_specs=P("row", "blk"), check_vma=False
    )
```

```python
import functools
import math

import jax
import jax.numpy as jnp
from jax import lax
from jax.experimental import pallas as pl
from jax.experimental.pallas import tpu as pltpu
from jax.sharding import PartitionSpec as P

NSTEPS = 5
MESH = pl.DeviceIdType.MESH


def product(a, b, lhs_dim=1):
    return lax.dot_general(
        a, b, (((lhs_dim,), (0,)), ((), ())), preferred_element_type=jnp.float32
    )


def split(a):
    high = a.astype(jnp.bfloat16)
    return high, (a - high.astype(jnp.float32)).astype(jnp.bfloat16)


def dot3(a, b, lhs_dim=1):
    high, low = a
    if lhs_dim == 0:
        n = high.shape[1]
        both = product(jnp.concatenate([high, low], axis=1), b[0], 0)
        return both[:n] + (both[n:] + product(high, b[1], 0))
    half = high.shape[0] // 2
    blocks = []
    for rows in (slice(0, half), slice(half, 2 * half)):
        both = product(jnp.concatenate([high[rows], low[rows]], axis=0), b[0])
        blocks.append(both[:half] + (both[half:] + product(high[rows], b[1])))
    return jnp.concatenate(blocks, axis=0)


def eye(n):
    rows = lax.broadcasted_iota(jnp.int32, (n, n), 0)
    columns = lax.broadcasted_iota(jnp.int32, (n, n), 1)
    return rows == columns


def diagonals(a):
    kept = jnp.where(eye(a.shape[0]), a, 0.0)
    return jnp.sum(kept, axis=1, keepdims=True), jnp.sum(kept, axis=0, keepdims=True)


class Solve:
    def __init__(self, starts):
        self.eye = jnp.where(eye(starts[0].shape[0]), 1.5, 0.0)
        y = [0.25 * m for m in starts]
        self.z = [self.eye - m for m in y]
        self.f = self.z_split = [split(z) for z in self.z]
        self.y = [dot3(f, split(m)) for f, m in zip(self.f, y)]
        self.y_split = [split(m) for m in self.y]

    def factors(self):
        self.f = [split(self.eye - dot3(y, z)) for y, z in zip(self.y_split, self.z_split)]

    def step(self):
        self.factors()
        self.z = [dot3(f, z) for f, z in zip(self.f, self.z_split)]
        self.z_split = [split(z) for z in self.z]
        self.y = [dot3(f, y) for f, y in zip(self.f, self.y_split)]
        self.y_split = [split(y) for y in self.y]


def half_of(a, second, axis):
    n = a.shape[axis] // 2
    first = lax.slice_in_dim(a, 0, n, axis=axis)
    return jnp.where(second, lax.slice_in_dim(a, n, 2 * n, axis=axis), first)


def kernel(
    blk_devices, z_devices,
    x_hbm, out_ref,
    x_ref, moved, gram_local, gram_core, gram_sum, gram_parts, gram_shard, gram_full, grams,
    cross_local, cross_core, cross_sum, cross_parts, cross_shard, cross, mixed_local, mixed_core,
    here_sem, load_sem, x_send, x_recv, gc_send, gc_recv, gz_send, gz_recv, ga_send, ga_recv,
    straight_send, across_send, gx_recv, cc_send, cc_recv, cz_send, cz_recv, ca_send, ca_recv, cf_send, cf_recv,
):
    k = lax.axis_index("blk")
    row = lax.axis_index("row")
    z = row // 2
    core = row % 2
    is_first = k == 0
    is_last = k == blk_devices - 1
    up = jnp.minimum(k + 1, blk_devices - 1)
    down = jnp.maximum(k - 1, 0)
    up_slot = jnp.where(is_last, 1, 0)
    down_slot = jnp.where(is_first, 0, 1)
    second = (k == 1, jnp.logical_not(is_last))
    half_width = x_ref.shape[1] // 2
    g_half = gram_local.shape[0] // 2
    g_part = half_width // z_devices
    g_parts = [(0, g_part + 8)] + [(8 + n * g_part, g_part) for n in range(1, z_devices)]
    c_half = cross_local.shape[0]
    c_part = c_half // z_devices
    middle = z_devices // 2
    lower_side = z < middle
    far_first = sorted(range(1, z_devices), key=lambda t: -min(t, z_devices - t))

    def peer(blk, t, other=False):
        return {"blk": blk, "row": lax.rem(z + t, z_devices) * 2 + (1 - core if other else core)}

    sibling = peer(k, 0, True)

    def remote(src, dst, send, recv, device):
        return pltpu.make_async_remote_copy(
            src_ref=src, dst_ref=dst, send_sem=send, recv_sem=recv,
            device_id=device, device_id_type=MESH,
        )

    def wait_for(ref, sem):
        pltpu.make_async_copy(ref, ref, sem).wait()

    def rows_at(start, size):
        return pl.ds(pl.multiple_of(start, 8), size)

    def either(condition, yes, no):
        pl.when(condition)(lambda: yes() and None)
        pl.when(jnp.logical_not(condition))(lambda: no() and None)

    def signal(sem, device):
        pl.semaphore_signal(sem, inc=1, device_id=device, device_id_type=MESH)

    load = pltpu.make_async_copy(x_hbm, x_ref, load_sem)
    load.start()

    barrier = pltpu.get_barrier_semaphore()
    for edge, blk in ((is_last, up), (is_first, down)):
        for other in (False, True):
            pl.when(jnp.logical_not(edge))(functools.partial(signal, barrier, peer(blk, 0, other)))
    signal(barrier, sibling)
    for t in range(z_devices - 1, 0, -1):
        pl.when(z + t < z_devices)(functools.partial(signal, barrier, peer(k, t)))
    neighbours = 2 - is_first.astype(jnp.int32) - is_last.astype(jnp.int32)

    load.wait()
    x_split = split(x_ref[...])
    g = dot3(x_split, x_split, 0)
    block_rows = lax.broadcasted_iota(jnp.int32, (half_width, half_width), 0)
    block_columns = lax.broadcasted_iota(jnp.int32, (half_width, half_width), 1)
    gram_local[:half_width] = g[:half_width, half_width:]
    gram_local[half_width:g_half] = jnp.zeros((8, half_width), jnp.float32)
    gram_local[g_half : g_half + half_width] = jnp.where(
        block_rows >= block_columns, g[:half_width, :half_width], g[half_width:, half_width:]
    )
    gram_local[g_half + half_width :] = jnp.broadcast_to(diagonals(g[half_width:, half_width:])[1], (8, half_width))

    pl.semaphore_wait(barrier, z + 1 + 2 * neighbours)

    for t in range(z_devices - 1, 0, -1):
        pl.when(z - t >= 0)(functools.partial(signal, here_sem.at[t - 1], peer(k, z_devices - t)))

    gc = remote(gram_local.at[rows_at((1 - core) * g_half, g_half)], gram_core, gc_send, gc_recv, sibling)
    gc.start()

    x_up = remote(x_ref, moved.at[up_slot], x_send.at[0], x_recv.at[up_slot], peer(up, 0))
    x_down = remote(x_ref, moved.at[down_slot], x_send.at[1], x_recv.at[down_slot], peer(down, 0))
    either(is_last, pltpu.make_async_copy(x_ref, moved.at[1], x_recv.at[1]).start, x_up.start)
    either(is_first, pltpu.make_async_copy(x_ref, moved.at[0], x_recv.at[0]).start, x_down.start)


    def to_others(src, dst, send, recv):
        for there in range(z_devices):
            copy = remote(src, dst, send, recv, {"blk": k, "row": there * 2 + core})
            pl.when(z != there)(copy.start)

    def tree(terms):
        while len(terms) > 1:
            terms = [a + b for a, b in zip(terms[::2], terms[1::2])]
        return terms[0]

    gc.wait_recv()
    gram_sum[...] = gram_local[rows_at(core * g_half, g_half)] + gram_core[...]
    for owner in sorted(range(z_devices), key=lambda n: -min(n, z_devices - n)):

        @pl.when(z < owner)
        def _(owner=owner):
            pl.semaphore_wait(here_sem.at[owner - z - 1], 1)

        t = lax.rem(owner - z + z_devices, z_devices)
        start, size = g_parts[owner]
        copy = remote(
            gram_sum.at[pl.ds(start, size)], gram_parts.at[jnp.maximum(t - 1, 0), pl.ds(0, size)], gz_send, gz_recv,
            {"blk": k, "row": owner * 2 + core},
        )
        pl.when(z != owner)(copy.start)

    def own_part(start, size):
        wait_for(grams.at[0, pl.ds(0, (z_devices - 1) * size)], gz_recv)
        gram_shard[:size] = tree(
            [gram_sum[pl.ds(start, size)]] + [gram_parts[n, :size] for n in range(z_devices - 1)]
        )
        src, dst = gram_shard.at[pl.ds(0, size)], gram_full.at[pl.ds(start, size)]
        sem = ga_recv.at[jnp.where(lower_side, 0, 1)]
        pltpu.make_async_copy(src, dst, sem).start()
        to_others(src, dst, ga_send, sem)

    cc = remote(cross_local, cross_core, cc_send, cc_recv, sibling)

    def gram_sum_part():
        either(
            z == 0,
            functools.partial(own_part, *g_parts[0]),
            lambda: own_part(pl.multiple_of(8 + z * g_part, 8), g_part),
        )

    def cross_part():
        for slot in range(2):
            wait_for(moved.at[slot], x_recv.at[slot])
        b_split = split(moved[1])
        a_half = [half_of(moved[0], core == which, 1) for which in (0, 1)]
        cross_local[...] = dot3(split(a_half[0]), b_split, 0)
        cc.start()
        cross_sum[...] = dot3(split(a_half[1]), b_split, 0)
    either(
        lower_side,
        lambda: (cross_part(), gram_sum_part()),
        lambda: (gram_sum_part(), cross_part()),
    )

    cc.wait_recv()
    cross_sum[...] += cross_core[...]
    for owner in sorted(range(z_devices), key=lambda n: -min(n, z_devices - n)):
        t = lax.rem(owner - z + z_devices, z_devices)
        copy = remote(
            cross_sum.at[pl.ds(owner * c_part, c_part)], cross_parts.at[jnp.maximum(t - 1, 0)], cz_send, cz_recv,
            {"blk": k, "row": owner * 2 + core},
        )
        pl.when(z != owner)(copy.start)

    def forward(side):
        start = g_parts[side * middle][0]
        size = (g_parts[middle][0], g_half - g_parts[middle][0])[side]
        src = gram_full.at[pl.ds(start, size)]
        there = rows_at(core * g_half + start, size)
        wait_for(src, ga_recv.at[side])
        for n, (edge, blk, slot, own_slot) in enumerate(((is_last, up, up_slot, 1), (is_first, down, down_slot, 0))):
            dst = grams.at[slot, there]
            straight = remote(src, dst, straight_send.at[n], gx_recv.at[slot], peer(blk, 0))
            stays = pltpu.make_async_copy(src, grams.at[own_slot, there], gx_recv.at[own_slot])
            either(edge, stays.start, straight.start)
            remote(src, dst, across_send, gx_recv.at[slot], peer(blk, 0, True)).start()

    either(lower_side, lambda: (forward(0), forward(1)), lambda: (forward(1), forward(0)))

    wait_for(cross_parts, cz_recv)
    cross_shard[...] = tree([cross_sum[rows_at(z * c_part, c_part)]] + [cross_parts[n] for n in range(z_devices - 1)])
    c_mine = rows_at(z * c_part, c_part)
    to_others(cross_shard, cross.at[c_mine], ca_send, ca_recv)
    pltpu.make_async_copy(cross_shard, cross.at[c_mine], ca_recv).start()

    for slot in range(2):
        wait_for(grams.at[slot], gx_recv.at[slot])
    diag_rows, roots_columns, scaled = [], [], []
    for slot in range(2):
        upper = grams[slot, pl.ds(0, half_width)]
        packed = grams[slot, pl.ds(g_half, half_width)]
        corner = jnp.where(block_rows < block_columns, packed, packed.T)
        corner = jnp.where(block_rows == block_columns, grams[slot, pl.ds(g_half + half_width, 1)], corner)
        full = jnp.concatenate(
            [
                jnp.concatenate([jnp.where(block_rows >= block_columns, packed, packed.T), upper], axis=1),
                jnp.concatenate([upper.T, corner], axis=1),
            ],
            axis=0,
        )
        column, line = diagonals(full)
        diag_rows.append(line)
        roots_columns.append(lax.rsqrt(column))
        scaled.append(full * roots_columns[slot] * lax.rsqrt(line))
    first = Solve(scaled)
    for _ in range(NSTEPS - 2):
        first.step()
    first.factors()
    zs, t_rows, its, ul = [], [], [], []
    moved_split = [split(moved[slot]) for slot in range(2)]
    for n in range(2):
        z_half = dot3(first.f[n], split(half_of(first.z[n], second[n], 1)))
        y_half = dot3(first.f[n], split(half_of(first.y[n], second[n], 1)))
        own = 4.0 * dot3(split(z_half), split(y_half), 0)
        t_column, t_row = diagonals(own)
        it_row = lax.rsqrt(t_row)
        t_rows.append(t_row)
        z_unit = z_half * it_row
        zs.append(z_unit)
        its.append(own * lax.rsqrt(t_column) * it_row)
        ul.append(split(z_unit * roots_columns[n]))
    diag2 = jnp.concatenate([half_of(diag_rows[n], second[n], 1) * t_rows[n] for n in range(2)], axis=1)
    ends = math.sqrt(0.5) * jnp.sqrt(0.5 * diag2)
    root_row = lax.rsqrt(diag_rows[1])

    gc.wait_send()
    cc.wait_send()
    wait_for(cross_parts, cz_send)
    wait_for(cross_parts, ca_send)

    def own_sent(gz_rows, ga_rows):
        wait_for(grams.at[0, pl.ds(0, gz_rows)], gz_send)
        wait_for(grams.at[0, pl.ds(0, ga_rows)], ga_send)

    others = z_devices - 1
    either(
        z == 0,
        lambda: own_sent(others * g_part, others * (g_part + 8)),
        lambda: own_sent(others * g_part + 8, others * g_part),
    )
    wait_for(grams.at[0], across_send)
    for n, (edge, copy) in enumerate(((is_last, x_up), (is_first, x_down))):

        @pl.when(jnp.logical_not(edge))
        def _(n=n, copy=copy):
            copy.wait_send()
            wait_for(gram_full, straight_send.at[n])

    z_rows = split(half_of(zs[0], core == 1, 0))
    z_other = split(zs[1])
    roots_half = half_of(roots_columns[0], core == 1, 0)
    wait_for(cross, ca_recv)
    turned = dot3(split(cross[...] * roots_half * root_row), z_other)
    mixed_local[...] = dot3(z_rows, split(turned), 0)
    cf = remote(mixed_local, mixed_core, cf_send, cf_recv, sibling)
    cf.start()
    cf.wait_recv()
    off = mixed_local[...] + mixed_core[...]
    scaled2 = jnp.concatenate(
        [jnp.concatenate([its[0], off], axis=1), jnp.concatenate([off.T, its[1]], axis=1)], axis=0
    )
    last = Solve([scaled2])
    last.step()
    ul = [split(dot3(moved_split[n], ul[n])) for n in range(2)]
    ul = [jnp.concatenate([ul[0][p], ul[1][p]], axis=1) for p in range(2)]
    for _ in range(NSTEPS - 3):
        last.step()
    last.factors()
    almost = dot3(ul, last.z_split[0])
    out_ref[...] = dot3(split(almost), last.f[0]) * ends
    cf.wait_send()


def shards(blk_devices, z_devices, x):
    rows, width = x.shape
    half = width // 2
    dma = pltpu.SemaphoreType.DMA
    g_half, c_half = half + 8, width // 2
    g_part = half // z_devices + 8
    others = z_devices - 1
    vmem = lambda *shape: pltpu.VMEM(shape, jnp.float32)
    return pl.pallas_call(
        functools.partial(kernel, blk_devices, z_devices),
        out_shape=jax.ShapeDtypeStruct(x.shape, jnp.float32),
        in_specs=[pl.BlockSpec(memory_space=pltpu.MemorySpace.HBM)],
        out_specs=pl.BlockSpec(memory_space=pltpu.VMEM),
        scratch_shapes=[
            vmem(rows, width), vmem(2, rows, width),
            vmem(2 * g_half, half), vmem(g_half, half), vmem(g_half, half),
            vmem(others, g_part, half), vmem(g_part, half), vmem(g_half, half), vmem(2, 2 * g_half, half),
            vmem(c_half, width), vmem(c_half, width), vmem(c_half, width),
            vmem(others, c_half // z_devices, width), vmem(c_half // z_devices, width), vmem(c_half, width),
            vmem(half, half), vmem(half, half),
            pltpu.SemaphoreType.REGULAR((others,)), dma, dma((2,)), dma((2,)), dma, dma, dma, dma, dma, dma((2,)),
            dma((2,)), dma, dma((2,)), dma, dma, dma, dma, dma, dma, dma, dma,
        ],
        compiler_params=pltpu.CompilerParams(
            collective_id=0, has_side_effects=True, vmem_limit_bytes=32 * 1024 * 1024
        ),
        cost_estimate=pl.CostEstimate(
            flops=40 * 3 * 2 * width**3, bytes_accessed=8 * rows * width, transcendentals=4096
        ),
        name="rotate_pairs",
    )(pltpu.with_memory_space_constraint(x, pltpu.MemorySpace.HBM))


def solution(mesh):
    run = functools.partial(shards, mesh.shape["blk"], mesh.shape["row"] // 2)
    return jax.shard_map(
        run, mesh=mesh, in_specs=(P("row", "blk"),), out_specs=P("row", "blk"), check_vma=False
    )
```
